32 devices in a mesh: dp: 8 (over y, x, core), cent: 4 (over z).
Axes of the slice: x: 2, y: 2, z: 4, core: 2. Of those that a mesh axis runs over, the one named last changes fastest.
Arguments:
- points: bfloat16 [16384, 1024], P(('dp', 'cent')), may hold values from -8 to 8
- fine_assign: int32 [16384], P(('dp', 'cent')), may hold values from 0 to 4095, as said below
- coarse_assign: int32 [4096], P(('dp', 'cent')), may hold values from 0 to 4095, as said below
Outputs:
- spread: float32 [16384], P(('dp', 'cent'))
- fine_centroids: bfloat16 [4096, 1024], P(('dp', 'cent'))
- coarse_centroids: bfloat16 [4096, 1024], P('cent')
The draws below stay inside these ranges and needn't reach their ends.
Inputs may be any that keep to these rules, and one draw needn't show every extreme that they name: `fine_assign`: devices are numbered with dp slowest; device s holds points s * 512 to (s + 1) * 512 - 1 and fine centroids s * 128 to (s + 1) * 128 - 1. At most 32 of the points of one device are assigned into any one block b * 128 to (b + 1) * 128 - 1 of fine centroids, and in every draw some block receives exactly 32 points from every device. `coarse_assign`: the 128 fine centroids of one device name at most 64 coarse centroids of any one block c * 1024 to (c + 1) * 1024 - 1, and in every draw some block receives exactly 64 from every device.
All inputs are finite; a program needn't handle non-finite values.
Results may differ from the reference program's by a relative error of at most 0.014.
Values may be sent and summed in bfloat16 or wider, within the bound.
A program may use at most 64 MiB of HBM per device.

```python
import jax
import jax.numpy as jnp
from jax import lax

D = 1024
P_DEV = 512
FINE_DEV = 128
COARSE = 4096
SOURCES = 32
POINTS = 16384
FINE = 4096
CAP = 32
COARSE_BLOCK = 1024
CAP2 = 64
N_DP = 8
N_CENT = 4


def bounded_targets(key, sources, targets, capacity, per_source):
    busiest = jax.random.randint(jax.random.fold_in(key, 0), (), 0, targets)

    def single_source(source):
        source_key = jax.random.fold_in(key, source + 1)
        permuted = jax.random.permutation(jax.random.fold_in(source_key, 1), targets * capacity)
        owners = jnp.arange(targets * capacity, dtype=jnp.int32) // capacity
        scores = jnp.where(owners == busiest, -1, permuted.astype(jnp.int32))
        ranking = jnp.argsort(scores, stable=True)
        chosen = owners[ranking][:per_source]
        shuffled = jax.random.permutation(jax.random.fold_in(source_key, 2), per_source)
        return chosen[shuffled]
    return jax.vmap(single_source)(jnp.arange(sources, dtype=jnp.int32)).reshape(-1)


def skewed_local(key, count, span):
    first = jax.random.randint(jax.random.fold_in(key, 1), (count,), 0, span)
    second = jax.random.randint(jax.random.fold_in(key, 2), (count,), 0, span)
    return first * second // (span - 1)


def assignments(key):
    fine_key = jax.random.fold_in(key, 101)
    fine_owner = bounded_targets(jax.random.fold_in(fine_key, 1), SOURCES, SOURCES, CAP, P_DEV)
    fine_ids = fine_owner * FINE_DEV + skewed_local(jax.random.fold_in(fine_key, 2), POINTS, FINE_DEV)
    coarse_key = jax.random.fold_in(key, 202)
    coarse_owner = bounded_targets(jax.random.fold_in(coarse_key, 1), SOURCES, N_CENT, CAP2, FINE_DEV)
    coarse_ids = coarse_owner * COARSE_BLOCK + skewed_local(jax.random.fold_in(coarse_key, 2), FINE, COARSE_BLOCK)
    return (fine_ids.astype(jnp.int32), coarse_ids.astype(jnp.int32))


def draw_fine_assign(key, part):
    fine_ids, coarse_ids = assignments(key)
    return fine_ids


def draw_coarse_assign(key, part):
    fine_ids, coarse_ids = assignments(key)
    return coarse_ids


def draw_points(key, part):
    fine_ids, coarse_ids = assignments(key)
    key = jax.random.fold_in(key, 7)
    coarse_table = jnp.clip(jax.random.normal(jax.random.fold_in(key, 1), (COARSE, D), jnp.float32), -4.0, 4.0)
    own_table = jnp.clip(jax.random.normal(jax.random.fold_in(key, 2), (FINE, D), jnp.float32), -4.0, 4.0)
    fine_table = 0.6 * coarse_table[coarse_ids] + 0.8 * own_table
    noise = jnp.clip(jax.random.normal(jax.random.fold_in(key, 3), (POINTS, D), jnp.float32), -4.0, 4.0)
    return (0.8 * fine_table[fine_ids] + 0.6 * noise).astype(jnp.bfloat16)


def setup_inputs(seed: int = 0) -> dict:
    key_list = jax.random.split(jax.random.key(seed), 4)
    points = draw_points(jax.random.fold_in(key_list[3], 71), 0)
    fine_assign = draw_fine_assign(jax.random.fold_in(key_list[3], 71), 0)
    coarse_assign = draw_coarse_assign(jax.random.fold_in(key_list[3], 71), 0)
    return {"points": points, "fine_assign": fine_assign, "coarse_assign": coarse_assign}


def reference(points, fine_assign, coarse_assign):
    span = P_DEV * N_CENT

    def accumulate(carry, index):
        start = (index * span).astype(jnp.int32)
        rows = lax.dynamic_slice_in_dim(points, start, span, 0).astype(jnp.float32)
        labels = lax.dynamic_slice_in_dim(fine_assign, start, span, 0)
        totals, tallies = carry
        totals = totals + jax.ops.segment_sum(rows, labels, FINE)
        tallies = tallies + jax.ops.segment_sum(jnp.ones((span,), jnp.float32), labels, FINE)
        return (totals, tallies), None

    start_carry = (jnp.zeros((FINE, D), jnp.float32), jnp.zeros((FINE,), jnp.float32))
    (fine_sums, fine_counts), unused = lax.scan(accumulate, start_carry, jnp.arange(N_DP, dtype=jnp.int32))
    fine_centroids = (fine_sums / jnp.maximum(fine_counts, 1.0)[:, None]).astype(jnp.bfloat16)

    def deviation(index):
        start = (index * span).astype(jnp.int32)
        rows = lax.dynamic_slice_in_dim(points, start, span, 0).astype(jnp.float32)
        labels = lax.dynamic_slice_in_dim(fine_assign, start, span, 0)
        nearest = fine_centroids[labels].astype(jnp.float32)
        return jnp.mean(jnp.square(rows - nearest), axis=-1)

    spread = lax.map(deviation, jnp.arange(N_DP, dtype=jnp.int32)).reshape(POINTS)
    coarse_sums = jax.ops.segment_sum(fine_centroids.astype(jnp.float32), coarse_assign, COARSE)
    coarse_counts = jax.ops.segment_sum(jnp.ones((FINE,), jnp.float32), coarse_assign, COARSE)
    coarse_centroids = (coarse_sums / jnp.maximum(coarse_counts, 1.0)[:, None]).astype(jnp.bfloat16)
    return spread, fine_centroids, coarse_centroids
```

```python
import functools

import jax
import jax.numpy as jnp
from jax import lax
from jax.experimental import pallas as pl
from jax.experimental.pallas import tpu as pltpu
from jax.sharding import PartitionSpec as P

COARSE = 4096
CHUNKS = 4
MESH = pl.DeviceIdType.MESH
F32 = jnp.float32
BF16 = jnp.bfloat16
I32 = jnp.int32


def log2(n):
    assert n & (n - 1) == 0
    return n.bit_length() - 1


def iota(shape, dim):
    return lax.broadcasted_iota(I32, shape, dim)


def to_col(row, rows):
    shape = (rows, row.shape[1])
    same = iota(shape, 0) == iota(shape, 1)
    return jnp.sum(jnp.where(same, row, 0.0), axis=1, keepdims=True)


def to_row(col, lanes):
    shape = (col.shape[0], lanes)
    same = iota(shape, 0) == iota(shape, 1)
    return jnp.sum(jnp.where(same, col, 0.0), axis=0, keepdims=True)


def kernel(cfg, *refs):
    (n_dp, n_cent, p_rows, fine, width, w, cap, cap2, block) = cfg
    (points, fa, ca, spread_out, fine_out, coarse_out,
     sel, send, recv, mt, m, pf, cz, gr, g,
     ids_s, ids_r, lab, glab, cnt_s, cnt_r, sp_s, sp_r, acc) = refs[:24]
    bits = log2(n_cent)
    rs_out = refs[24 : 24 + bits]
    rs_in = refs[24 + bits : 24 + 2 * bits]
    (a_ss, a_rs, rs_ss, rs_rs, ag_ss, ag_rs, g_ss, g_rs,
     id_ss, id_rs, lab_ss, lab_rs, cnt_ss, cnt_rs, gl_ss, gl_rs, sp_ss, sp_rs) = refs[24 + 2 * bits :]
    chunks = width // w
    group = n_cent * fine
    rows2 = n_cent * cap2
    lanes = max(cap, 128)
    me = lax.axis_index("dp")
    mz = lax.axis_index("cent")

    def reverse(z):
        return sum(((z // (1 << b)) % 2) * (1 << (bits - 1 - b)) for b in range(bits))

    place = reverse(mz)

    def at8(k):
        return pl.ds(pl.multiple_of(k * 8, 8), 8)

    def span(k, size):
        return pl.ds(pl.multiple_of(k * size, size), size)

    def dp_peer(j):
        return lax.rem(me + j, n_dp)

    def cent_peer(j):
        return lax.rem(mz + j, n_cent)

    started = []

    def copy(src, dst, ss, rs, d=None, z=None):
        made = pltpu.make_async_remote_copy(
            src_ref=src, dst_ref=dst, send_sem=ss, recv_sem=rs,
            device_id=(me if d is None else d, mz if z is None else z), device_id_type=MESH,
        )
        return made

    def go(*args, **kwargs):
        made = copy(*args, **kwargs)
        made.start()
        started.append(made)
        return made

    barrier = pltpu.get_barrier_semaphore()
    for j in range(1, n_dp):
        pl.semaphore_signal(barrier, inc=1, device_id=(dp_peer(j), mz), device_id_type=MESH)
    for j in range(1, n_cent):
        pl.semaphore_signal(barrier, inc=1, device_id=(me, cent_peer(j)), device_id_type=MESH)

    f_row = fa[...]
    d_row = (f_row >> log2(group)).astype(F32)
    z_row = (f_row & (group - 1)) >> log2(fine)
    p_row = (f_row & (fine - 1)) + sum(
        ((z_row >> b) & 1) << (bits - 1 - b + log2(fine)) for b in range(bits)
    )
    d_col = to_col(d_row, p_rows)
    p_col = to_col(p_row.astype(F32), p_rows)
    square = (p_rows, p_rows)
    earlier = jnp.logical_and(d_col == d_row, iota(square, 0) < iota(square, 1))
    rank_row = jnp.sum(jnp.where(earlier, 1.0, 0.0), axis=0, keepdims=True)
    rank_col = to_col(rank_row, p_rows)
    slot_row = d_row * cap + rank_row
    for k in range(n_dp):
        slots = (iota((cap, p_rows), 0) + k * cap).astype(F32)
        sel[pl.ds(k * cap, cap), :] = jnp.where(slots == slot_row, 1.0, 0.0).astype(BF16)

    pl.semaphore_wait(barrier, n_dp + n_cent - 2)

    lab[at8(place), :] = jnp.broadcast_to(ca[...], (8, fine))
    for j in range(1, n_cent):
        mine = lab.at[at8(place)]
        go(mine, mine, lab_ss.at[j], lab_rs.at[j], z=cent_peer(j))
    for c in range(chunks):
        moved = jnp.dot(sel[...], points[:, pl.ds(c * w, w)], preferred_element_type=F32)
        send[c] = moved.astype(BF16)
        for j in range(1, n_dp):
            go(send.at[c, span(dp_peer(j), cap)], recv.at[c, span(me, cap)],
               a_ss.at[c, j], a_rs.at[c, j], d=dp_peer(j))
        recv[c, span(me, cap), :] = send[c, span(me, cap), :]
        if c == 0:
            for k in range(n_dp):
                hit = jnp.where(d_col == k, rank_col, -1.0) == iota((p_rows, lanes), 1).astype(F32)
                row = jnp.sum(jnp.where(hit, p_col + 1.0, 0.0), axis=0, keepdims=True) - 1.0
                ids_s[pl.ds(k * 8, 8), :] = jnp.broadcast_to(row, (8, lanes))
            for j in range(1, n_dp):
                go(ids_s.at[at8(dp_peer(j))], ids_r.at[at8(me)], id_ss.at[j], id_rs.at[j], d=dp_peer(j))
            ids_r[at8(me), :] = ids_s[at8(me), :]

    for j in range(1, n_cent):
        copy(lab.at[at8(place)], lab.at[at8(reverse(cent_peer(n_cent - j)))],
             lab_ss.at[j], lab_rs.at[j], z=cent_peer(n_cent - j)).wait_recv()
    small = (fine, fine)
    before = iota(small, 0) < iota(small, 1)
    labels = jnp.zeros((1, rows2), F32)
    pick = []
    for k in range(n_cent):
        row = lab[pl.ds(k * 8, 1), :]
        inside = jnp.where((row >> log2(block)) == mz, 1.0, 0.0)
        inside_col = to_col(inside, fine)
        value_col = to_col((row & (block - 1)).astype(F32), fine)
        rank = jnp.sum(jnp.where(before, inside_col, 0.0), axis=0, keepdims=True)
        slot = jnp.where(inside > 0.0, rank + k * cap2, -1.0)
        slot_col = to_col(slot, fine)
        hit = slot_col == iota((fine, rows2), 1).astype(F32)
        labels = labels + jnp.sum(jnp.where(hit, value_col + 1.0, 0.0), axis=0, keepdims=True)
        pick.append(jnp.where(slot == iota((rows2, fine), 0).astype(F32), 1.0, 0.0).astype(BF16))
    glab[at8(me), :] = jnp.broadcast_to(labels - 1.0, (8, rows2))
    for j in range(1, n_dp):
        mine = glab.at[at8(me)]
        go(mine, mine, gl_ss.at[j], gl_rs.at[j], d=dp_peer(j))

    for j in range(1, n_dp):
        copy(ids_s.at[at8(me)], ids_r.at[at8(dp_peer(n_dp - j))],
             id_ss.at[j], id_rs.at[j], d=dp_peer(n_dp - j)).wait_recv()
    tally = jnp.zeros((1, group), F32)
    for k in range(n_dp):
        row = ids_r[pl.ds(k * 8, 1), :]
        col = to_col(row, cap)
        part = jnp.where(col == iota((cap, group), 1).astype(F32), 1.0, 0.0)
        mt[pl.ds(k * cap, cap), :] = part.astype(BF16)
        tally = tally + jnp.sum(part, axis=0, keepdims=True)
        if cap % 128 == 0:
            hit = row == iota((group, cap), 0).astype(F32)
            m[:, pl.ds(k * cap, cap)] = jnp.where(hit, 1.0, 0.0).astype(BF16)
    for k in range(n_cent):
        cnt_s[pl.ds(k * 8, 8), :] = jnp.broadcast_to(tally[:, k * fine : (k + 1) * fine], (8, fine))
    for j in range(1, n_cent):
        go(cnt_s.at[at8(reverse(cent_peer(j)))], cnt_r.at[pl.ds(j * 8, 8)],
           cnt_ss.at[j], cnt_rs.at[j], z=cent_peer(j))

    for j in range(1, n_dp):
        copy(glab.at[at8(me)], glab.at[at8(dp_peer(n_dp - j))],
             gl_ss.at[j], gl_rs.at[j], d=dp_peer(n_dp - j)).wait_recv()
    coarse_tally = jnp.zeros((block, 1), F32)
    for k in range(n_dp):
        row = glab[pl.ds(k * 8, 1), :]
        part = jnp.where(row == iota((block, rows2), 0).astype(F32), 1.0, 0.0)
        g[:, pl.ds(k * rows2, rows2)] = part.astype(BF16)
        coarse_tally = coarse_tally + jnp.sum(part, axis=1, keepdims=True)
    coarse_scale = jnp.maximum(coarse_tally, 1.0)

    for j in range(1, n_cent):
        copy(cnt_s.at[at8(place)], cnt_r.at[pl.ds(j * 8, 8)],
             cnt_ss.at[j], cnt_rs.at[j], z=cent_peer(n_cent - j)).wait_recv()
    total = cnt_s[at8(place), :]
    for j in range(1, n_cent):
        total = total + cnt_r[pl.ds(j * 8, 8), :]
    fine_scale = jnp.maximum(to_col(total[0:1, :], fine), 1.0)
    acc[...] = jnp.zeros_like(acc)

    def cent_partner(b):
        return mz + (1 - 2 * ((mz // (1 << b)) % 2)) * (1 << b)

    def keep(b):
        size = n_cent >> b
        return (place // size) * size

    def rs_parts(c, b):
        return (rs_out[b].at[c], rs_in[b].at[c], rs_ss.at[c, b], rs_rs.at[c, b])

    def rs_send(c, b):
        half = n_cent >> (b + 1)
        other = 2 * keep(b) + half - keep(b + 1)
        rs_out[b][c] = pf[c, pl.ds(pl.multiple_of(other * fine, fine), half * fine), :].astype(BF16)
        go(*rs_parts(c, b), z=cent_partner(b))

    def rs_add(c, b):
        half = n_cent >> (b + 1)
        copy(*rs_parts(c, b), z=cent_partner(b)).wait_recv()
        mine = pl.ds(pl.multiple_of(keep(b + 1) * fine, fine), half * fine)
        pf[c, mine, :] += rs_in[b][c].astype(F32)

    def ag_parts(c, b, sender_place):
        size = 1 << (bits - 1 - b)
        first = (sender_place // size) * size
        part = cz.at[c, pl.ds(pl.multiple_of(first * fine, fine), size * fine)]
        return (part, part, ag_ss.at[c, b], ag_rs.at[c, b])

    def ag_send(c, b):
        go(*ag_parts(c, b, place), z=cent_partner(b))

    def ag_wait(c, b):
        copy(*ag_parts(c, b, reverse(cent_partner(b))), z=cent_partner(b)).wait_recv()

    def sums(c):
        for j in range(1, n_dp):
            source = dp_peer(n_dp - j)
            copy(send.at[c, span(me, cap)], recv.at[c, span(source, cap)],
                 a_ss.at[c, j], a_rs.at[c, j], d=source).wait_recv()
        if cap % 128 == 0:
            pf[c] = jnp.dot(m[...], recv[c], preferred_element_type=F32)
        else:
            pf[c] = lax.dot_general(mt[...], recv[c], (((0,), (0,)), ((), ())),
                                    preferred_element_type=F32)
        rs_send(c, 0)

    def halve(b, c):
        rs_add(c, b - 1)
        rs_send(c, b)

    def centroids(c):
        rs_add(c, bits - 1)
        value = (pf[c, span(place, fine), :] / fine_scale).astype(BF16)
        cz[c, span(place, fine), :] = value
        fine_out[:, pl.ds(c * w, w)] = value
        ag_send(c, bits - 1)

    def double(b, c):
        ag_wait(c, b + 1)
        ag_send(c, b)

    def g_rows(c, d):
        return gr.at[c, span(d, rows2)]

    def g_args(c, k, d):
        return (g_rows(c, d), g_rows(c, d), g_ss.at[c, k], g_rs.at[c, k])

    if n_dp == 8:
        core = me % 2
        dx = (1 - 2 * ((me // 2) % 2)) * 2
        dy = (1 - 2 * ((me // 4) % 2)) * 4
        d1 = (1 - core) * dx + core * dy
        d2 = (1 - core) * dy + core * dx
        d3 = 1 - 2 * core

    def pick_rows(c):
        ag_wait(c, 0)
        mine = jnp.zeros((rows2, w), F32)
        for k in range(n_cent):
            mine = mine + jnp.dot(pick[k], cz[c, pl.ds(k * fine, fine), :], preferred_element_type=F32)
        gr[c, span(me, rows2), :] = mine.astype(BF16)
        if n_dp == 8:
            go(*g_args(c, 0, me), d=me + d1)
            go(*g_args(c, 1, me), d=me + d2)
            go(*g_args(c, 2, me), d=me + d3)
        else:
            for j in range(1, n_dp):
                go(*g_args(c, j, me), d=dp_peer(j))
        near = jnp.dot(mt[...], cz[c], preferred_element_type=F32)
        gap = jnp.square(recv[c].astype(F32) - near)
        acc[...] += sum(gap[:, i : i + 128] for i in range(0, w, 128))
        if c == chunks - 1:
            for k in range(n_dp):
                col = jnp.sum(acc[pl.ds(k * cap, cap), :], axis=1, keepdims=True) / width
                sp_s[pl.ds(k * 8, 8), :] = jnp.broadcast_to(to_row(col, lanes), (8, lanes))
            for j in range(1, n_dp):
                go(sp_s.at[at8(dp_peer(j))], sp_r.at[at8(me)], sp_ss.at[j], sp_rs.at[j], d=dp_peer(j))
            sp_r[at8(me), :] = sp_s[at8(me), :]

    def forward_one(c):
        if n_dp == 8:
            copy(*g_args(c, 0, me + d1), d=me + d1).wait_recv()
            go(*g_args(c, 3, me + d1), d=me + d2)
            go(*g_args(c, 4, me + d1), d=me + d3)
            copy(*g_args(c, 1, me + d2), d=me + d2).wait_recv()
            go(*g_args(c, 5, me + d2), d=me + d3)

    def forward_two(c):
        if n_dp == 8:
            copy(*g_args(c, 3, me + d1 + d2), d=me + d2).wait_recv()
            go(*g_args(c, 6, me + d1 + d2), d=me + d3)

    def finish(c):
        if n_dp == 8:
            copy(*g_args(c, 2, me + d3), d=me + d3).wait_recv()
            copy(*g_args(c, 4, me + d3 + d2), d=me + d3).wait_recv()
            copy(*g_args(c, 5, me + d3 + d1), d=me + d3).wait_recv()
            copy(*g_args(c, 6, me + d3 + d1 + d2), d=me + d3).wait_recv()
        else:
            for j in range(1, n_dp):
                source = dp_peer(n_dp - j)
                copy(*g_args(c, j, source), d=source).wait_recv()
        result = jnp.dot(g[...], gr[c], preferred_element_type=F32)
        coarse_out[:, pl.ds(c * w, w)] = (result / coarse_scale).astype(BF16)

    stages = [sums]
    stages += [functools.partial(halve, b) for b in range(1, bits)]
    stages += [centroids]
    stages += [functools.partial(double, b) for b in reversed(range(bits - 1))]
    stages += [pick_rows, forward_one, forward_two, finish]
    for tick in range(chunks + len(stages) - 1):
        for s in reversed(range(len(stages))):
            if 0 <= tick - s < chunks:
                stages[s](tick - s)

    for j in range(1, n_dp):
        source = dp_peer(n_dp - j)
        copy(sp_s.at[at8(me)], sp_r.at[at8(source)], sp_ss.at[j], sp_rs.at[j], d=source).wait_recv()
    spread = jnp.zeros((1, p_rows), F32)
    for k in range(n_dp):
        col = to_col(sp_r[pl.ds(k * 8, 1), :], cap)
        slots = (iota((cap, p_rows), 0) + k * cap).astype(F32)
        spread = spread + jnp.sum(jnp.where(slots == slot_row, col, 0.0), axis=0, keepdims=True)
    spread_out[...] = spread
    for made in started:
        made.wait_send()


def body(points, fine_assign, coarse_assign):
    n_dp = lax.axis_size("dp")
    n_cent = lax.axis_size("cent")
    p_rows, width = points.shape
    fine = coarse_assign.shape[0]
    sources = n_dp * n_cent
    cap = max(2, 2 * p_rows // sources) * n_cent
    cap2 = max(2, 2 * fine // n_cent)
    block = COARSE // n_cent
    w = width // CHUNKS
    bits = log2(n_cent)
    group, slots, rows2, lanes = n_cent * fine, n_dp * cap, n_cent * cap2, max(cap, 128)
    cfg = (n_dp, n_cent, p_rows, fine, width, w, cap, cap2, block)
    halves = [pltpu.VMEM((CHUNKS, (n_cent >> (b + 1)) * fine, w), BF16) for b in range(bits)]
    dma = pltpu.SemaphoreType.DMA
    scratch = [
        pltpu.VMEM((slots, p_rows), BF16),
        pltpu.VMEM((CHUNKS, slots, w), BF16),
        pltpu.VMEM((CHUNKS, slots, w), BF16),
        pltpu.VMEM((slots, group), BF16),
        pltpu.VMEM((group, slots) if cap % 128 == 0 else (16, 128), BF16),
        pltpu.VMEM((CHUNKS, group, w), F32),
        pltpu.VMEM((CHUNKS, group, w), BF16),
        pltpu.VMEM((CHUNKS, n_dp * rows2, w), BF16),
        pltpu.VMEM((block, n_dp * rows2), BF16),
        pltpu.VMEM((n_dp * 8, lanes), F32),
        pltpu.VMEM((n_dp * 8, lanes), F32),
        pltpu.VMEM((n_cent * 8, fine), I32),
        pltpu.VMEM((n_dp * 8, rows2), F32),
        pltpu.VMEM((n_cent * 8, fine), F32),
        pltpu.VMEM((n_cent * 8, fine), F32),
        pltpu.VMEM((n_dp * 8, lanes), F32),
        pltpu.VMEM((n_dp * 8, lanes), F32),
        pltpu.VMEM((slots, 128), F32),
        *halves,
        *halves,
        dma((CHUNKS, n_dp)), dma((CHUNKS, n_dp)),
        dma((CHUNKS, bits)), dma((CHUNKS, bits)),
        dma((CHUNKS, bits)), dma((CHUNKS, bits)),
        dma((CHUNKS, n_dp)), dma((CHUNKS, n_dp)),
        dma((n_dp,)), dma((n_dp,)),
        dma((n_cent,)), dma((n_cent,)),
        dma((n_cent,)), dma((n_cent,)),
        dma((n_dp,)), dma((n_dp,)),
        dma((n_dp,)), dma((n_dp,)),
    ]
    vmem = pl.BlockSpec(memory_space=pltpu.VMEM)
    spread, fine_centroids, coarse_centroids = pl.pallas_call(
        functools.partial(kernel, cfg),
        out_shape=(
            jax.ShapeDtypeStruct((1, p_rows), F32),
            jax.ShapeDtypeStruct((fine, width), BF16),
            jax.ShapeDtypeStruct((block, width), BF16),
        ),
        in_specs=[vmem] * 3,
        out_specs=(vmem,) * 3,
        scratch_shapes=scratch,
        compiler_params=pltpu.CompilerParams(
            collective_id=0, has_side_effects=True, vmem_limit_bytes=60 * 1024 * 1024
        ),
        cost_estimate=pl.CostEstimate(
            flops=2 * width * (slots * (p_rows + 2 * group) + block * n_dp * rows2),
            bytes_accessed=2 * width * (p_rows + fine + block),
            transcendentals=0,
        ),
    )(points, fine_assign.reshape(1, p_rows), coarse_assign.reshape(1, fine))
    return (spread.reshape(p_rows), fine_centroids, coarse_centroids)


def solution(mesh):
    placed = (P(("dp", "cent"), None), P(("dp", "cent")), P(("dp", "cent")))
    return jax.shard_map(
        body,
        mesh=mesh,
        in_specs=placed,
        out_specs=(P(("dp", "cent")), P(("dp", "cent"), None), P("cent", None)),
        check_vma=False,
    )
```

```python
import functools

import jax
import jax.numpy as jnp
from jax import lax
from jax.experimental import pallas as pl
from jax.experimental.pallas import tpu as pltpu
from jax.sharding import PartitionSpec as P

COARSE = 4096
CHUNKS = 4
MESH = pl.DeviceIdType.MESH
F32 = jnp.float32
BF16 = jnp.bfloat16
I32 = jnp.int32


def log2(n):
    assert n & (n - 1) == 0
    return n.bit_length() - 1


def iota(shape, dim):
    return lax.broadcasted_iota(I32, shape, dim)


def to_col(row, rows):
    shape = (rows, row.shape[1])
    same = iota(shape, 0) == iota(shape, 1)
    return jnp.sum(jnp.where(same, row, 0.0), axis=1, keepdims=True)


def to_row(col, lanes):
    shape = (col.shape[0], lanes)
    same = iota(shape, 0) == iota(shape, 1)
    return jnp.sum(jnp.where(same, col, 0.0), axis=0, keepdims=True)


def kernel(cfg, *refs):
    (n_dp, n_cent, p_rows, fine, width, w, cap, cap2, block) = cfg
    (points, fa, ca, spread_out, fine_out, coarse_out,
     sel, send, recv, mt, m, pf, cz, gr, g,
     ids_s, ids_r, lab, glab, cnt_s, cnt_r, sp_s, sp_r, acc) = refs[:24]
    bits = log2(n_cent)
    rs_out = refs[24 : 24 + bits]
    rs_in = refs[24 + bits : 24 + 2 * bits]
    (a_ss, a_rs, rs_ss, rs_rs, ag_ss, ag_rs, g_ss, g_rs,
     id_ss, id_rs, lab_ss, lab_rs, cnt_ss, cnt_rs, gl_ss, gl_rs, sp_ss, sp_rs) = refs[24 + 2 * bits :]
    chunks = width // w
    group = n_cent * fine
    rows2 = n_cent * cap2
    lanes = max(cap, 128)
    me = lax.axis_index("dp")
    mz = lax.axis_index("cent")

    def reverse(z):
        return sum(((z // (1 << b)) % 2) * (1 << (bits - 1 - b)) for b in range(bits))

    place = reverse(mz)

    def at8(k):
        return pl.ds(pl.multiple_of(k * 8, 8), 8)

    def span(k, size):
        return pl.ds(pl.multiple_of(k * size, size), size)

    def dp_peer(j):
        return lax.rem(me + j, n_dp)

    def cent_peer(j):
        return lax.rem(mz + j, n_cent)

    started = []

    def copy(src, dst, ss, rs, d=None, z=None):
        made = pltpu.make_async_remote_copy(
            src_ref=src, dst_ref=dst, send_sem=ss, recv_sem=rs,
            device_id=(me if d is None else d, mz if z is None else z), device_id_type=MESH,
        )
        return made

    def go(*args, **kwargs):
        made = copy(*args, **kwargs)
        made.start()
        started.append(made)
        return made

    barrier = pltpu.get_barrier_semaphore()
    for j in range(1, n_dp):
        pl.semaphore_signal(barrier, inc=1, device_id=(dp_peer(j), mz), device_id_type=MESH)
    for j in range(1, n_cent):
        pl.semaphore_signal(barrier, inc=1, device_id=(me, cent_peer(j)), device_id_type=MESH)

    f_row = fa[...]
    d_row = (f_row >> log2(group)).astype(F32)
    z_row = (f_row & (group - 1)) >> log2(fine)
    p_row = (f_row & (fine - 1)) + sum(
        ((z_row >> b) & 1) << (bits - 1 - b + log2(fine)) for b in range(bits)
    )
    d_col = to_col(d_row, p_rows)
    square = (p_rows, p_rows)
    earlier = jnp.logical_and(d_col == d_row, iota(square, 0) < iota(square, 1))
    rank_row = jnp.sum(jnp.where(earlier, 1.0, 0.0), axis=0, keepdims=True)
    slot_row = d_row * cap + rank_row
    for k in range(n_dp):
        slots = (iota((cap, p_rows), 0) + k * cap).astype(F32)
        sel[pl.ds(k * cap, cap), :] = jnp.where(slots == slot_row, 1.0, 0.0).astype(BF16)

    pl.semaphore_wait(barrier, n_dp + n_cent - 2)

    lab[at8(place), :] = jnp.broadcast_to(ca[...], (8, fine))
    for j in range(1, n_cent):
        mine = lab.at[at8(place)]
        go(mine, mine, lab_ss.at[j], lab_rs.at[j], z=cent_peer(j))
    def prepare(c):
        moved = jnp.dot(sel[...], points[:, pl.ds(c * w, w)], preferred_element_type=F32)
        send[c] = moved.astype(BF16)
        recv[c, span(me, cap), :] = send[c, span(me, cap), :]

    def dispatch(c):
        for j in range(1, n_dp):
            go(send.at[c, span(dp_peer(j), cap)], recv.at[c, span(me, cap)],
               a_ss.at[c, j], a_rs.at[c, j], d=dp_peer(j))

    prepare(0)
    dispatch(0)
    p_col = to_col(p_row.astype(F32), p_rows)
    rank_col = to_col(rank_row, p_rows)
    for k in range(n_dp):
        hit = jnp.where(d_col == k, rank_col, -1.0) == iota((p_rows, lanes), 1).astype(F32)
        row = jnp.sum(jnp.where(hit, p_col + 1.0, 0.0), axis=0, keepdims=True) - 1.0
        ids_s[pl.ds(k * 8, 8), :] = jnp.broadcast_to(row, (8, lanes))
    for j in range(1, n_dp):
        go(ids_s.at[at8(dp_peer(j))], ids_r.at[at8(me)], id_ss.at[j], id_rs.at[j], d=dp_peer(j))
    ids_r[at8(me), :] = ids_s[at8(me), :]
    for c in range(1, chunks):
        prepare(c)
        if c == 1:
            dispatch(1)

    for j in range(1, n_cent):
        copy(lab.at[at8(place)], lab.at[at8(reverse(cent_peer(n_cent - j)))],
             lab_ss.at[j], lab_rs.at[j], z=cent_peer(n_cent - j)).wait_recv()
    small = (fine, fine)
    before = iota(small, 0) < iota(small, 1)
    labels = jnp.zeros((1, rows2), F32)
    pick = []
    for k in range(n_cent):
        row = lab[pl.ds(k * 8, 1), :]
        inside = jnp.where((row >> log2(block)) == mz, 1.0, 0.0)
        inside_col = to_col(inside, fine)
        value_col = to_col((row & (block - 1)).astype(F32), fine)
        rank = jnp.sum(jnp.where(before, inside_col, 0.0), axis=0, keepdims=True)
        slot = jnp.where(inside > 0.0, rank + k * cap2, -1.0)
        slot_col = to_col(slot, fine)
        hit = slot_col == iota((fine, rows2), 1).astype(F32)
        labels = labels + jnp.sum(jnp.where(hit, value_col + 1.0, 0.0), axis=0, keepdims=True)
        pick.append(jnp.where(slot == iota((rows2, fine), 0).astype(F32), 1.0, 0.0).astype(BF16))
    glab[at8(me), :] = jnp.broadcast_to(labels - 1.0, (8, rows2))
    for j in range(1, n_dp):
        mine = glab.at[at8(me)]
        go(mine, mine, gl_ss.at[j], gl_rs.at[j], d=dp_peer(j))

    for j in range(1, n_dp):
        copy(ids_s.at[at8(me)], ids_r.at[at8(dp_peer(n_dp - j))],
             id_ss.at[j], id_rs.at[j], d=dp_peer(n_dp - j)).wait_recv()
    tally = jnp.zeros((1, group), F32)
    for k in range(n_dp):
        row = ids_r[pl.ds(k * 8, 1), :]
        col = to_col(row, cap)
        part = jnp.where(col == iota((cap, group), 1).astype(F32), 1.0, 0.0)
        mt[pl.ds(k * cap, cap), :] = part.astype(BF16)
        tally = tally + jnp.sum(part, axis=0, keepdims=True)
        if cap % 128 == 0:
            hit = row == iota((group, cap), 0).astype(F32)
            m[:, pl.ds(k * cap, cap)] = jnp.where(hit, 1.0, 0.0).astype(BF16)
    for k in range(n_cent):
        cnt_s[pl.ds(k * 8, 8), :] = jnp.broadcast_to(tally[:, k * fine : (k + 1) * fine], (8, fine))
    for j in range(1, n_cent):
        go(cnt_s.at[at8(reverse(cent_peer(j)))], cnt_r.at[pl.ds(j * 8, 8)],
           cnt_ss.at[j], cnt_rs.at[j], z=cent_peer(j))

    for j in range(1, n_dp):
        copy(glab.at[at8(me)], glab.at[at8(dp_peer(n_dp - j))],
             gl_ss.at[j], gl_rs.at[j], d=dp_peer(n_dp - j)).wait_recv()
    coarse_tally = jnp.zeros((block, 1), F32)
    for k in range(n_dp):
        row = glab[pl.ds(k * 8, 1), :]
        part = jnp.where(row == iota((block, rows2), 0).astype(F32), 1.0, 0.0)
        g[:, pl.ds(k * rows2, rows2)] = part.astype(BF16)
        coarse_tally = coarse_tally + jnp.sum(part, axis=1, keepdims=True)
    coarse_scale = jnp.maximum(coarse_tally, 1.0)

    for j in range(1, n_cent):
        copy(cnt_s.at[at8(place)], cnt_r.at[pl.ds(j * 8, 8)],
             cnt_ss.at[j], cnt_rs.at[j], z=cent_peer(n_cent - j)).wait_recv()
    total = cnt_s[at8(place), :]
    for j in range(1, n_cent):
        total = total + cnt_r[pl.ds(j * 8, 8), :]
    fine_scale = jnp.maximum(to_col(total[0:1, :], fine), 1.0)
    acc[...] = jnp.zeros_like(acc)

    def cent_partner(b):
        return mz + (1 - 2 * ((mz // (1 << b)) % 2)) * (1 << b)

    def keep(b):
        size = n_cent >> b
        return (place // size) * size

    def rs_parts(c, b):
        return (rs_out[b].at[c], rs_in[b].at[c], rs_ss.at[c, b], rs_rs.at[c, b])

    def rs_send(c, b):
        half = n_cent >> (b + 1)
        other = 2 * keep(b) + half - keep(b + 1)
        rs_out[b][c] = pf[c, pl.ds(pl.multiple_of(other * fine, fine), half * fine), :].astype(BF16)
        go(*rs_parts(c, b), z=cent_partner(b))

    def rs_add(c, b):
        half = n_cent >> (b + 1)
        copy(*rs_parts(c, b), z=cent_partner(b)).wait_recv()
        mine = pl.ds(pl.multiple_of(keep(b + 1) * fine, fine), half * fine)
        pf[c, mine, :] += rs_in[b][c].astype(F32)

    def ag_send(c):
        mine = cz.at[c, span(place, fine)]
        for j in range(1, n_cent):
            go(mine, mine, ag_ss.at[c, j], ag_rs.at[c, j], z=cent_peer(j))

    def ag_wait(c):
        for j in range(1, n_cent):
            source = cent_peer(n_cent - j)
            theirs = cz.at[c, span(reverse(source), fine)]
            copy(theirs, theirs, ag_ss.at[c, j], ag_rs.at[c, j], z=source).wait_recv()

    def sums(c):
        for j in range(1, n_dp):
            source = dp_peer(n_dp - j)
            copy(send.at[c, span(me, cap)], recv.at[c, span(source, cap)],
                 a_ss.at[c, j], a_rs.at[c, j], d=source).wait_recv()
        if c + 2 < chunks:
            dispatch(c + 2)
        if cap % 128 == 0:
            pf[c] = jnp.dot(m[...], recv[c], preferred_element_type=F32)
        else:
            pf[c] = lax.dot_general(mt[...], recv[c], (((0,), (0,)), ((), ())),
                                    preferred_element_type=F32)
        rs_send(c, 0)

    def halve(b, c):
        rs_add(c, b - 1)
        rs_send(c, b)

    def centroids(c):
        rs_add(c, bits - 1)
        value = (pf[c, span(place, fine), :] / fine_scale).astype(BF16)
        cz[c, span(place, fine), :] = value
        fine_out[:, pl.ds(c * w, w)] = value
        ag_send(c)

    def g_rows(c, d):
        return gr.at[c, span(d, rows2)]

    def g_args(c, k, d):
        return (g_rows(c, d), g_rows(c, d), g_ss.at[c, k], g_rs.at[c, k])

    if n_dp == 8:
        core = me % 2
        dx = (1 - 2 * ((me // 2) % 2)) * 2
        dy = (1 - 2 * ((me // 4) % 2)) * 4
        d1 = (1 - core) * dx + core * dy
        d2 = (1 - core) * dy + core * dx
        d3 = 1 - 2 * core

    def pick_rows(c):
        ag_wait(c)
        mine = jnp.zeros((rows2, w), F32)
        for k in range(n_cent):
            mine = mine + jnp.dot(pick[k], cz[c, pl.ds(k * fine, fine), :], preferred_element_type=F32)
        gr[c, span(me, rows2), :] = mine.astype(BF16)
        if n_dp == 8:
            go(*g_args(c, 0, me), d=me + d1)
            go(*g_args(c, 1, me), d=me + d2)
            go(*g_args(c, 2, me), d=me + d3)
        else:
            for j in range(1, n_dp):
                go(*g_args(c, j, me), d=dp_peer(j))
        near = jnp.dot(mt[...], cz[c], preferred_element_type=F32)
        gap = jnp.square(recv[c].astype(F32) - near)
        acc[...] += sum(gap[:, i : i + 128] for i in range(0, w, 128))
        if c == chunks - 1:
            for k in range(n_dp):
                col = jnp.sum(acc[pl.ds(k * cap, cap), :], axis=1, keepdims=True) / width
                sp_s[pl.ds(k * 8, 8), :] = jnp.broadcast_to(to_row(col, lanes), (8, lanes))
            for j in range(1, n_dp):
                go(sp_s.at[at8(dp_peer(j))], sp_r.at[at8(me)], sp_ss.at[j], sp_rs.at[j], d=dp_peer(j))
            sp_r[at8(me), :] = sp_s[at8(me), :]

    def forward_one(c):
        if n_dp == 8:
            copy(*g_args(c, 0, me + d1), d=me + d1).wait_recv()
            go(*g_args(c, 3, me + d1), d=me + d2)
            go(*g_args(c, 4, me + d1), d=me + d3)
            copy(*g_args(c, 1, me + d2), d=me + d2).wait_recv()
            go(*g_args(c, 5, me + d2), d=me + d3)

    def forward_two(c):
        if n_dp == 8:
            copy(*g_args(c, 3, me + d1 + d2), d=me + d2).wait_recv()
            go(*g_args(c, 6, me + d1 + d2), d=me + d3)

    def finish(c):
        if n_dp == 8:
            copy(*g_args(c, 2, me + d3), d=me + d3).wait_recv()
            copy(*g_args(c, 4, me + d3 + d2), d=me + d3).wait_recv()
            copy(*g_args(c, 5, me + d3 + d1), d=me + d3).wait_recv()
            copy(*g_args(c, 6, me + d3 + d1 + d2), d=me + d3).wait_recv()
        else:
            for j in range(1, n_dp):
                source = dp_peer(n_dp - j)
                copy(*g_args(c, j, source), d=source).wait_recv()
        result = jnp.dot(g[...], gr[c], preferred_element_type=F32)
        coarse_out[:, pl.ds(c * w, w)] = (result / coarse_scale).astype(BF16)

    stages = [sums]
    stages += [functools.partial(halve, b) for b in range(1, bits)]
    stages += [centroids]
    stages += [pick_rows, forward_one, forward_two, finish]
    for tick in range(chunks + len(stages) - 1):
        for s in reversed(range(len(stages))):
            if 0 <= tick - s < chunks:
                stages[s](tick - s)

    for j in range(1, n_dp):
        source = dp_peer(n_dp - j)
        copy(sp_s.at[at8(me)], sp_r.at[at8(source)], sp_ss.at[j], sp_rs.at[j], d=source).wait_recv()
    spread = jnp.zeros((1, p_rows), F32)
    for k in range(n_dp):
        col = to_col(sp_r[pl.ds(k * 8, 1), :], cap)
        slots = (iota((cap, p_rows), 0) + k * cap).astype(F32)
        spread = spread + jnp.sum(jnp.where(slots == slot_row, col, 0.0), axis=0, keepdims=True)
    spread_out[...] = spread
    for made in started:
        made.wait_send()


def place_results(*refs):
    n = (len(refs) - 1) // 2
    moves = [pltpu.make_async_copy(refs[i], refs[n + i], refs[-1].at[i]) for i in range(n)]
    for move in moves:
        move.start()
    for move in moves:
        move.wait()


def body(points, fine_assign, coarse_assign):
    n_dp = lax.axis_size("dp")
    n_cent = lax.axis_size("cent")
    p_rows, width = points.shape
    fine = coarse_assign.shape[0]
    sources = n_dp * n_cent
    cap = max(2, 2 * p_rows // sources) * n_cent
    cap2 = max(2, 2 * fine // n_cent)
    block = COARSE // n_cent
    w = width // CHUNKS
    bits = log2(n_cent)
    group, slots, rows2, lanes = n_cent * fine, n_dp * cap, n_cent * cap2, max(cap, 128)
    cfg = (n_dp, n_cent, p_rows, fine, width, w, cap, cap2, block)
    halves = [pltpu.VMEM((CHUNKS, (n_cent >> (b + 1)) * fine, w), BF16) for b in range(bits)]
    dma = pltpu.SemaphoreType.DMA
    scratch = [
        pltpu.VMEM((slots, p_rows), BF16),
        pltpu.VMEM((CHUNKS, slots, w), BF16),
        pltpu.VMEM((CHUNKS, slots, w), BF16),
        pltpu.VMEM((slots, group), BF16),
        pltpu.VMEM((group, slots) if cap % 128 == 0 else (16, 128), BF16),
        pltpu.VMEM((CHUNKS, group, w), F32),
        pltpu.VMEM((CHUNKS, group, w), BF16),
        pltpu.VMEM((CHUNKS, n_dp * rows2, w), BF16),
        pltpu.VMEM((block, n_dp * rows2), BF16),
        pltpu.VMEM((n_dp * 8, lanes), F32),
        pltpu.VMEM((n_dp * 8, lanes), F32),
        pltpu.VMEM((n_cent * 8, fine), I32),
        pltpu.VMEM((n_dp * 8, rows2), F32),
        pltpu.VMEM((n_cent * 8, fine), F32),
        pltpu.VMEM((n_cent * 8, fine), F32),
        pltpu.VMEM((n_dp * 8, lanes), F32),
        pltpu.VMEM((n_dp * 8, lanes), F32),
        pltpu.VMEM((slots, 128), F32),
        *halves,
        *halves,
        dma((CHUNKS, n_dp)), dma((CHUNKS, n_dp)),
        dma((CHUNKS, bits)), dma((CHUNKS, bits)),
        dma((CHUNKS, n_cent)), dma((CHUNKS, n_cent)),
        dma((CHUNKS, n_dp)), dma((CHUNKS, n_dp)),
        dma((n_dp,)), dma((n_dp,)),
        dma((n_cent,)), dma((n_cent,)),
        dma((n_cent,)), dma((n_cent,)),
        dma((n_dp,)), dma((n_dp,)),
        dma((n_dp,)), dma((n_dp,)),
    ]
    vmem = pl.BlockSpec(memory_space=pltpu.VMEM)
    results = pl.pallas_call(
        functools.partial(kernel, cfg),
        out_shape=(
            jax.ShapeDtypeStruct((1, p_rows), F32),
            jax.ShapeDtypeStruct((fine, width), BF16),
            jax.ShapeDtypeStruct((block, width), BF16),
        ),
        in_specs=[vmem] * 3,
        out_specs=(vmem,) * 3,
        scratch_shapes=scratch,
        compiler_params=pltpu.CompilerParams(
            collective_id=0, has_side_effects=True, vmem_limit_bytes=60 * 1024 * 1024
        ),
        cost_estimate=pl.CostEstimate(
            flops=2 * width * (slots * (p_rows + 2 * group) + block * n_dp * rows2),
            bytes_accessed=2 * width * (p_rows + fine + block),
            transcendentals=0,
        ),
    )(points, fine_assign.reshape(1, p_rows), coarse_assign.reshape(1, fine))
    anywhere = pl.BlockSpec(memory_space=pl.ANY)
    spread, fine_centroids, coarse_centroids = pl.pallas_call(
        place_results,
        out_shape=tuple(jax.ShapeDtypeStruct(r.shape, r.dtype) for r in results),
        in_specs=[anywhere] * 3,
        out_specs=(anywhere,) * 3,
        scratch_shapes=[dma((3,))],
    )(*results)
    return (spread.reshape(p_rows), fine_centroids, coarse_centroids)


def solution(mesh):
    placed = (P(("dp", "cent"), None), P(("dp", "cent")), P(("dp", "cent")))
    return jax.shard_map(
        body,
        mesh=mesh,
        in_specs=placed,
        out_specs=(P(("dp", "cent")), P(("dp", "cent"), None), P("cent", None)),
        check_vma=False,
    )
```

```python
import functools

import jax
import jax.numpy as jnp
from jax import lax
from jax.experimental import pallas as pl
from jax.experimental.pallas import tpu as pltpu
from jax.sharding import PartitionSpec as P

COARSE = 4096
CHUNKS = 8
AHEAD = 3
PARTS = 4
MESH = pl.DeviceIdType.MESH
F32 = jnp.float32
BF16 = jnp.bfloat16
I32 = jnp.int32


def log2(n):
    assert n & (n - 1) == 0
    return n.bit_length() - 1


def iota(shape, dim):
    return lax.broadcasted_iota(I32, shape, dim)


def to_col(row, rows):
    shape = (rows, row.shape[1])
    same = iota(shape, 0) == iota(shape, 1)
    return jnp.sum(jnp.where(same, row, 0.0), axis=1, keepdims=True)


def to_row(col, lanes):
    shape = (col.shape[0], lanes)
    same = iota(shape, 0) == iota(shape, 1)
    return jnp.sum(jnp.where(same, col, 0.0), axis=0, keepdims=True)


def kernel(cfg, *refs):
    (n_dp, n_cent, p_rows, fine, width, w, cap, cap2, block) = cfg
    (points, fa, ca, spread_out, fine_out, coarse_out,
     sel, send, recv, mt, m, pf, cz, gr, g,
     ids_s, ids_r, lab, glab, cnt_s, cnt_r, sp_s, sp_r, acc) = refs[:24]
    bits = log2(n_cent)
    rs_out = refs[24 : 24 + bits]
    rs_in = refs[24 + bits : 24 + 2 * bits]
    (a_ss, a_rs, rs_ss, rs_rs, ag_ss, ag_rs, g_ss, g_rs,
     id_ss, id_rs, lab_ss, lab_rs, cnt_ss, cnt_rs, gl_ss, gl_rs, sp_ss, sp_rs) = refs[24 + 2 * bits :]
    chunks = width // w
    group = n_cent * fine
    live = bits + 1
    rows2 = n_cent * cap2
    lanes = max(cap, 128)
    me = lax.axis_index("dp")
    mz = lax.axis_index("cent")

    def reverse(z):
        return sum(((z // (1 << b)) % 2) * (1 << (bits - 1 - b)) for b in range(bits))

    place = reverse(mz)

    def at8(k):
        return pl.ds(pl.multiple_of(k * 8, 8), 8)

    def span(k, size):
        return pl.ds(pl.multiple_of(k * size, size), size)

    def dp_peer(j):
        return lax.rem(me + j, n_dp)

    def cent_peer(j):
        return lax.rem(mz + j, n_cent)

    started = []

    def copy(src, dst, ss, rs, d=None, z=None):
        made = pltpu.make_async_remote_copy(
            src_ref=src, dst_ref=dst, send_sem=ss, recv_sem=rs,
            device_id=(me if d is None else d, mz if z is None else z), device_id_type=MESH,
        )
        return made

    def go(*args, **kwargs):
        made = copy(*args, **kwargs)
        made.start()
        started.append(made)
        return made

    barrier = pltpu.get_barrier_semaphore()
    for j in range(1, n_dp):
        pl.semaphore_signal(barrier, inc=1, device_id=(dp_peer(j), mz), device_id_type=MESH)
    for j in range(1, n_cent):
        pl.semaphore_signal(barrier, inc=1, device_id=(me, cent_peer(j)), device_id_type=MESH)

    f_row = fa[...]
    d_row = (f_row >> log2(group)).astype(F32)
    z_row = (f_row & (group - 1)) >> log2(fine)
    p_row = (f_row & (fine - 1)) + sum(
        ((z_row >> b) & 1) << (bits - 1 - b + log2(fine)) for b in range(bits)
    )
    d_col = to_col(d_row, p_rows)
    square = (p_rows, p_rows)
    earlier = jnp.logical_and(d_col == d_row, iota(square, 0) < iota(square, 1))
    rank_row = jnp.sum(jnp.where(earlier, 1.0, 0.0), axis=0, keepdims=True)
    slot_row = d_row * cap + rank_row
    for k in range(n_dp):
        slots = (iota((cap, p_rows), 0) + k * cap).astype(F32)
        sel[pl.ds(k * cap, cap), :] = jnp.where(slots == slot_row, 1.0, 0.0).astype(BF16)

    pl.semaphore_wait(barrier, n_dp + n_cent - 2)

    lab[at8(place), :] = jnp.broadcast_to(ca[...], (8, fine))
    for j in range(1, n_cent):
        mine = lab.at[at8(place)]
        go(mine, mine, lab_ss.at[j], lab_rs.at[j], z=cent_peer(j))
    def prepare(c):
        moved = jnp.dot(sel[...], points[:, pl.ds(c * w, w)], preferred_element_type=F32)
        send[c] = moved.astype(BF16)
        recv[c, span(me, cap), :] = send[c, span(me, cap), :]

    def dispatch(c):
        for j in range(1, n_dp):
            go(send.at[c, span(dp_peer(j), cap)], recv.at[c, span(me, cap)],
               a_ss.at[c, j], a_rs.at[c, j], d=dp_peer(j))

    prepare(0)
    dispatch(0)
    p_col = to_col(p_row.astype(F32), p_rows)
    rank_col = to_col(rank_row, p_rows)
    for k in range(n_dp):
        hit = jnp.where(d_col == k, rank_col, -1.0) == iota((p_rows, lanes), 1).astype(F32)
        row = jnp.sum(jnp.where(hit, p_col + 1.0, 0.0), axis=0, keepdims=True) - 1.0
        ids_s[pl.ds(k * 8, 8), :] = jnp.broadcast_to(row, (8, lanes))
    for j in range(1, n_dp):
        go(ids_s.at[at8(dp_peer(j))], ids_r.at[at8(me)], id_ss.at[j], id_rs.at[j], d=dp_peer(j))
    ids_r[at8(me), :] = ids_s[at8(me), :]
    for c in range(1, chunks):
        prepare(c)
        if c < AHEAD:
            dispatch(c)

    for j in range(1, n_cent):
        copy(lab.at[at8(place)], lab.at[at8(reverse(cent_peer(n_cent - j)))],
             lab_ss.at[j], lab_rs.at[j], z=cent_peer(n_cent - j)).wait_recv()
    small = (fine, fine)
    before = iota(small, 0) < iota(small, 1)
    labels = jnp.zeros((1, rows2), F32)
    pick = []
    for k in range(n_cent):
        row = lab[pl.ds(k * 8, 1), :]
        inside = jnp.where((row >> log2(block)) == mz, 1.0, 0.0)
        inside_col = to_col(inside, fine)
        value_col = to_col((row & (block - 1)).astype(F32), fine)
        rank = jnp.sum(jnp.where(before, inside_col, 0.0), axis=0, keepdims=True)
        slot = jnp.where(inside > 0.0, rank + k * cap2, -1.0)
        slot_col = to_col(slot, fine)
        hit = slot_col == iota((fine, rows2), 1).astype(F32)
        labels = labels + jnp.sum(jnp.where(hit, value_col + 1.0, 0.0), axis=0, keepdims=True)
        pick.append(jnp.where(slot == iota((rows2, fine), 0).astype(F32), 1.0, 0.0).astype(BF16))
    glab[at8(me), :] = jnp.broadcast_to(labels - 1.0, (8, rows2))
    for j in range(1, n_dp):
        mine = glab.at[at8(me)]
        go(mine, mine, gl_ss.at[j], gl_rs.at[j], d=dp_peer(j))

    for j in range(1, n_dp):
        copy(ids_s.at[at8(me)], ids_r.at[at8(dp_peer(n_dp - j))],
             id_ss.at[j], id_rs.at[j], d=dp_peer(n_dp - j)).wait_recv()
    tally = jnp.zeros((1, group), F32)
    for k in range(n_dp):
        row = ids_r[pl.ds(k * 8, 1), :]
        col = to_col(row, cap)
        part = jnp.where(col == iota((cap, group), 1).astype(F32), 1.0, 0.0)
        mt[pl.ds(k * cap, cap), :] = part.astype(BF16)
        tally = tally + jnp.sum(part, axis=0, keepdims=True)
        if cap % 128 == 0:
            hit = row == iota((group, cap), 0).astype(F32)
            m[:, pl.ds(k * cap, cap)] = jnp.where(hit, 1.0, 0.0).astype(BF16)
    for k in range(n_cent):
        cnt_s[pl.ds(k * 8, 8), :] = jnp.broadcast_to(tally[:, k * fine : (k + 1) * fine], (8, fine))
    for j in range(1, n_cent):
        go(cnt_s.at[at8(reverse(cent_peer(j)))], cnt_r.at[pl.ds(j * 8, 8)],
           cnt_ss.at[j], cnt_rs.at[j], z=cent_peer(j))

    acc[...] = jnp.zeros_like(acc)

    def fine_counts():
        for j in range(1, n_cent):
            copy(cnt_s.at[at8(place)], cnt_r.at[pl.ds(j * 8, 8)],
                 cnt_ss.at[j], cnt_rs.at[j], z=cent_peer(n_cent - j)).wait_recv()
        total = cnt_s[at8(place), :]
        for j in range(1, n_cent):
            total = total + cnt_r[pl.ds(j * 8, 8), :]
        fine_scale = jnp.maximum(to_col(total[0:1, :], fine), 1.0)
        return fine_scale

    def coarse_members():
        for j in range(1, n_dp):
            copy(glab.at[at8(me)], glab.at[at8(dp_peer(n_dp - j))],
                 gl_ss.at[j], gl_rs.at[j], d=dp_peer(n_dp - j)).wait_recv()
        coarse_tally = jnp.zeros((block, 1), F32)
        for k in range(n_dp):
            row = glab[pl.ds(k * 8, 1), :]
            part = jnp.where(row == iota((block, rows2), 0).astype(F32), 1.0, 0.0)
            g[:, pl.ds(k * rows2, rows2)] = part.astype(BF16)
            coarse_tally = coarse_tally + jnp.sum(part, axis=1, keepdims=True)
        coarse_scale = jnp.maximum(coarse_tally, 1.0)
        return coarse_scale

    def cent_partner(b):
        return mz + (1 - 2 * ((mz // (1 << b)) % 2)) * (1 << b)

    def keep(b):
        size = n_cent >> b
        return (place // size) * size

    def rs_parts(c, b):
        return (rs_out[b].at[c], rs_in[b].at[c], rs_ss.at[c, b], rs_rs.at[c, b])

    def rs_send(c, b):
        half = n_cent >> (b + 1)
        other = 2 * keep(b) + half - keep(b + 1)
        rs_out[b][c] = pf[c % live, pl.ds(pl.multiple_of(other * fine, fine), half * fine), :].astype(BF16)
        go(*rs_parts(c, b), z=cent_partner(b))

    def rs_add(c, b):
        half = n_cent >> (b + 1)
        copy(*rs_parts(c, b), z=cent_partner(b)).wait_recv()
        mine = pl.ds(pl.multiple_of(keep(b + 1) * fine, fine), half * fine)
        pf[c % live, mine, :] += rs_in[b][c].astype(F32)

    def ag_send(c):
        mine = cz.at[c, span(place, fine)]
        for j in range(1, n_cent):
            go(mine, mine, ag_ss.at[c, j], ag_rs.at[c, j], z=cent_peer(j))

    def ag_wait(c):
        for j in range(1, n_cent):
            source = cent_peer(n_cent - j)
            theirs = cz.at[c, span(reverse(source), fine)]
            copy(theirs, theirs, ag_ss.at[c, j], ag_rs.at[c, j], z=source).wait_recv()

    def sums(c):
        for j in range(1, n_dp):
            source = dp_peer(n_dp - j)
            copy(send.at[c, span(me, cap)], recv.at[c, span(source, cap)],
                 a_ss.at[c, j], a_rs.at[c, j], d=source).wait_recv()
        if c + AHEAD < chunks:
            dispatch(c + AHEAD)
        if cap % 128 == 0:
            pf[c % live] = jnp.dot(m[...], recv[c], preferred_element_type=F32)
        else:
            pf[c % live] = lax.dot_general(mt[...], recv[c], (((0,), (0,)), ((), ())),
                                    preferred_element_type=F32)
        rs_send(c, 0)

    def halve(b, c):
        rs_add(c, b - 1)
        rs_send(c, b)

    def centroids(c):
        rs_add(c, bits - 1)
        value = (pf[c % live, span(place, fine), :] / fine_scale).astype(BF16)
        cz[c, span(place, fine), :] = value
        fine_out[:, pl.ds(c * w, w)] = value
        ag_send(c)

    def g_rows(c, d):
        return gr.at[c, span(d, rows2)]

    def g_args(c, k, d):
        return (g_rows(c, d), g_rows(c, d), g_ss.at[c, k], g_rs.at[c, k])

    if n_dp == 8:
        core = me % 2
        dx = (1 - 2 * ((me // 2) % 2)) * 2
        dy = (1 - 2 * ((me // 4) % 2)) * 4
        d1 = (1 - core) * dx + core * dy
        d2 = (1 - core) * dy + core * dx
        d3 = 1 - 2 * core

    def pick_rows(c):
        ag_wait(c)
        mine = jnp.zeros((rows2, w), F32)
        for k in range(n_cent):
            mine = mine + jnp.dot(pick[k], cz[c, pl.ds(k * fine, fine), :], preferred_element_type=F32)
        gr[c, span(me, rows2), :] = mine.astype(BF16)
        if n_dp == 8:
            go(*g_args(c, 0, me), d=me + d1)
            go(*g_args(c, 1, me), d=me + d2)
            go(*g_args(c, 2, me), d=me + d3)
        else:
            for j in range(1, n_dp):
                go(*g_args(c, j, me), d=dp_peer(j))
        near = jnp.dot(mt[...], cz[c], preferred_element_type=F32)
        gap = jnp.square(recv[c].astype(F32) - near)
        acc[...] += sum(gap[:, i : i + 128] for i in range(0, w, 128))
        if c == chunks - 1:
            for k in range(n_dp):
                col = jnp.sum(acc[pl.ds(k * cap, cap), :], axis=1, keepdims=True) / width
                sp_s[pl.ds(k * 8, 8), :] = jnp.broadcast_to(to_row(col, lanes), (8, lanes))
            for j in range(1, n_dp):
                go(sp_s.at[at8(dp_peer(j))], sp_r.at[at8(me)], sp_ss.at[j], sp_rs.at[j], d=dp_peer(j))
            sp_r[at8(me), :] = sp_s[at8(me), :]

    def forward_one(c):
        if n_dp == 8:
            copy(*g_args(c, 0, me + d1), d=me + d1).wait_recv()
            go(*g_args(c, 3, me + d1), d=me + d2)
            go(*g_args(c, 4, me + d1), d=me + d3)
            copy(*g_args(c, 1, me + d2), d=me + d2).wait_recv()
            go(*g_args(c, 5, me + d2), d=me + d3)

    def forward_two(c):
        if n_dp == 8:
            copy(*g_args(c, 3, me + d1 + d2), d=me + d2).wait_recv()
            go(*g_args(c, 6, me + d1 + d2), d=me + d3)

    def finish(c):
        if n_dp == 8:
            copy(*g_args(c, 2, me + d3), d=me + d3).wait_recv()
            copy(*g_args(c, 4, me + d3 + d2), d=me + d3).wait_recv()
            copy(*g_args(c, 5, me + d3 + d1), d=me + d3).wait_recv()
            copy(*g_args(c, 6, me + d3 + d1 + d2), d=me + d3).wait_recv()
        else:
            for j in range(1, n_dp):
                source = dp_peer(n_dp - j)
                copy(*g_args(c, j, source), d=source).wait_recv()
        result = jnp.dot(g[...], gr[c], preferred_element_type=F32)
        coarse_out[:, pl.ds(c * w, w)] = (result / coarse_scale).astype(BF16)

    stages = [sums]
    stages += [functools.partial(halve, b) for b in range(1, bits)]
    stages += [centroids]
    stages += [pick_rows, forward_one, forward_two, finish]
    for tick in range(chunks + len(stages) - 1):
        for s in reversed(range(len(stages))):
            if 0 <= tick - s < chunks:
                stages[s](tick - s)
        if tick == 0:
            fine_scale = fine_counts()
        if tick == 1:
            coarse_scale = coarse_members()

    for j in range(1, n_dp):
        source = dp_peer(n_dp - j)
        copy(sp_s.at[at8(me)], sp_r.at[at8(source)], sp_ss.at[j], sp_rs.at[j], d=source).wait_recv()
    spread = jnp.zeros((1, p_rows), F32)
    for k in range(n_dp):
        col = to_col(sp_r[pl.ds(k * 8, 1), :], cap)
        slots = (iota((cap, p_rows), 0) + k * cap).astype(F32)
        spread = spread + jnp.sum(jnp.where(slots == slot_row, col, 0.0), axis=0, keepdims=True)
    spread_out[...] = spread
    for made in started:
        made.wait_send()


def place_results(*refs):
    n = 3
    ins, outs, held, (sem_in, sem_out) = refs[:n], refs[n : 2 * n], refs[2 * n : 3 * n], refs[3 * n :]
    parts = []
    for i in (2, 1, 0):
        count = PARTS if i == 2 else 1
        rows = ins[i].shape[0] // count
        parts += [(i, pl.ds(k * rows, rows)) for k in range(count)]
    first = [
        pltpu.make_async_copy(ins[i].at[at], held[i].at[at], sem_in.at[k])
        for k, (i, at) in enumerate(parts)
    ]
    second = [
        pltpu.make_async_copy(held[i].at[at], outs[i].at[at], sem_out.at[k])
        for k, (i, at) in enumerate(parts)
    ]
    for move in first:
        move.start()
    for k, move in enumerate(first):
        move.wait()
        second[k].start()
    for move in second:
        move.wait()


def body(points, fine_assign, coarse_assign):
    n_dp = lax.axis_size("dp")
    n_cent = lax.axis_size("cent")
    p_rows, width = points.shape
    fine = coarse_assign.shape[0]
    sources = n_dp * n_cent
    cap = max(2, 2 * p_rows // sources) * n_cent
    cap2 = max(2, 2 * fine // n_cent)
    block = COARSE // n_cent
    w = width // CHUNKS
    bits = log2(n_cent)
    group, slots, rows2, lanes = n_cent * fine, n_dp * cap, n_cent * cap2, max(cap, 128)
    cfg = (n_dp, n_cent, p_rows, fine, width, w, cap, cap2, block)
    halves = [pltpu.VMEM((CHUNKS, (n_cent >> (b + 1)) * fine, w), BF16) for b in range(bits)]
    dma = pltpu.SemaphoreType.DMA
    scratch = [
        pltpu.VMEM((slots, p_rows), BF16),
        pltpu.VMEM((CHUNKS, slots, w), BF16),
        pltpu.VMEM((CHUNKS, slots, w), BF16),
        pltpu.VMEM((slots, group), BF16),
        pltpu.VMEM((group, slots) if cap % 128 == 0 else (16, 128), BF16),
        pltpu.VMEM((bits + 1, group, w), F32),
        pltpu.VMEM((CHUNKS, group, w), BF16),
        pltpu.VMEM((CHUNKS, n_dp * rows2, w), BF16),
        pltpu.VMEM((block, n_dp * rows2), BF16),
        pltpu.VMEM((n_dp * 8, lanes), F32),
        pltpu.VMEM((n_dp * 8, lanes), F32),
        pltpu.VMEM((n_cent * 8, fine), I32),
        pltpu.VMEM((n_dp * 8, rows2), F32),
        pltpu.VMEM((n_cent * 8, fine), F32),
        pltpu.VMEM((n_cent * 8, fine), F32),
        pltpu.VMEM((n_dp * 8, lanes), F32),
        pltpu.VMEM((n_dp * 8, lanes), F32),
        pltpu.VMEM((slots, 128), F32),
        *halves,
        *halves,
        dma((CHUNKS, n_dp)), dma((CHUNKS, n_dp)),
        dma((CHUNKS, bits)), dma((CHUNKS, bits)),
        dma((CHUNKS, n_cent)), dma((CHUNKS, n_cent)),
        dma((CHUNKS, n_dp)), dma((CHUNKS, n_dp)),
        dma((n_dp,)), dma((n_dp,)),
        dma((n_cent,)), dma((n_cent,)),
        dma((n_cent,)), dma((n_cent,)),
        dma((n_dp,)), dma((n_dp,)),
        dma((n_dp,)), dma((n_dp,)),
    ]
    vmem = pl.BlockSpec(memory_space=pltpu.VMEM)
    results = pl.pallas_call(
        functools.partial(kernel, cfg),
        out_shape=(
            jax.ShapeDtypeStruct((1, p_rows), F32),
            jax.ShapeDtypeStruct((fine, width), BF16),
            jax.ShapeDtypeStruct((block, width), BF16),
        ),
        in_specs=[vmem] * 3,
        out_specs=(vmem,) * 3,
        scratch_shapes=scratch,
        compiler_params=pltpu.CompilerParams(
            collective_id=0, has_side_effects=True, vmem_limit_bytes=60 * 1024 * 1024
        ),
        cost_estimate=pl.CostEstimate(
            flops=2 * width * (slots * (p_rows + 2 * group) + block * n_dp * rows2),
            bytes_accessed=2 * width * (p_rows + fine + block),
            transcendentals=0,
        ),
    )(points, fine_assign.reshape(1, p_rows), coarse_assign.reshape(1, fine))
    anywhere = pl.BlockSpec(memory_space=pl.ANY)
    spread, fine_centroids, coarse_centroids = pl.pallas_call(
        place_results,
        out_shape=tuple(jax.ShapeDtypeStruct(r.shape, r.dtype) for r in results),
        in_specs=[anywhere] * 3,
        out_specs=(anywhere,) * 3,
        scratch_shapes=[
            *(pltpu.VMEM(r.shape, r.dtype) for r in results),
            dma((PARTS + 2,)),
            dma((PARTS + 2,)),
        ],
    )(*results)
    return (spread.reshape(p_rows), fine_centroids, coarse_centroids)


def solution(mesh):
    placed = (P(("dp", "cent"), None), P(("dp", "cent")), P(("dp", "cent")))
    return jax.shard_map(
        body,
        mesh=mesh,
        in_specs=placed,
        out_specs=(P(("dp", "cent")), P(("dp", "cent"), None), P("cent", None)),
        check_vma=False,
    )
```

```python
import functools

import jax
import jax.numpy as jnp
from jax import lax
from jax.experimental import pallas as pl
from jax.experimental.pallas import tpu as pltpu
from jax.sharding import PartitionSpec as P

COARSE = 4096
AHEAD = 4
PARTS = 4
MESH = pl.DeviceIdType.MESH
F32 = jnp.float32
BF16 = jnp.bfloat16
I32 = jnp.int32


def log2(n):
    assert n & (n - 1) == 0
    return n.bit_length() - 1


def iota(shape, dim):
    return lax.broadcasted_iota(I32, shape, dim)


def to_col(row, rows):
    shape = (rows, row.shape[1])
    same = iota(shape, 0) == iota(shape, 1)
    return jnp.sum(jnp.where(same, row, 0.0), axis=1, keepdims=True)


def to_row(col, lanes):
    shape = (col.shape[0], lanes)
    same = iota(shape, 0) == iota(shape, 1)
    return jnp.sum(jnp.where(same, col, 0.0), axis=0, keepdims=True)


def kernel(cfg, *refs):
    (n_dp, n_cent, p_rows, fine, width, widths, cap, cap2, block) = cfg
    (points, fa, ca, spread_out, fine_out, coarse_out,
     sel, mt, m, pf, g,
     ids_s, ids_r, lab, glab, cnt_s, cnt_r, sp_s, sp_r, acc) = refs[:20]
    bits = log2(n_cent)
    chunks = len(widths)
    starts = [sum(widths[:c]) for c in range(chunks)]
    lists = [refs[20 + k * chunks : 20 + (k + 1) * chunks] for k in range(4 + 2 * bits)]
    send, recv, cz, gr = lists[:4]
    rs_out, rs_in = lists[4 : 4 + bits], lists[4 + bits :]
    (a_ss, a_rs, rs_ss, rs_rs, ag_ss, ag_rs, g_ss, g_rs,
     id_ss, id_rs, lab_ss, lab_rs, cnt_ss, cnt_rs, gl_ss, gl_rs, sp_ss, sp_rs) = refs[20 + (4 + 2 * bits) * chunks :]
    group = n_cent * fine
    live = bits + 1
    rows2 = n_cent * cap2
    lanes = max(cap, 128)
    me = lax.axis_index("dp")
    mz = lax.axis_index("cent")

    def reverse(z):
        return sum(((z // (1 << b)) % 2) * (1 << (bits - 1 - b)) for b in range(bits))

    place = reverse(mz)

    def at8(k):
        return pl.ds(pl.multiple_of(k * 8, 8), 8)

    def span(k, size):
        return pl.ds(pl.multiple_of(k * size, size), size)

    def dp_peer(j):
        return lax.rem(me + j, n_dp)

    def cent_peer(j):
        return lax.rem(mz + j, n_cent)

    started = []

    def copy(src, dst, ss, rs, d=None, z=None):
        made = pltpu.make_async_remote_copy(
            src_ref=src, dst_ref=dst, send_sem=ss, recv_sem=rs,
            device_id=(me if d is None else d, mz if z is None else z), device_id_type=MESH,
        )
        return made

    def go(*args, **kwargs):
        made = copy(*args, **kwargs)
        made.start()
        started.append(made)
        return made

    barrier = pltpu.get_barrier_semaphore()
    for j in range(1, n_dp):
        pl.semaphore_signal(barrier, inc=1, device_id=(dp_peer(j), mz), device_id_type=MESH)
    for j in range(1, n_cent):
        pl.semaphore_signal(barrier, inc=1, device_id=(me, cent_peer(j)), device_id_type=MESH)

    f_row = fa[...]
    d_row = (f_row >> log2(group)).astype(F32)
    z_row = (f_row & (group - 1)) >> log2(fine)
    p_row = (f_row & (fine - 1)) + sum(
        ((z_row >> b) & 1) << (bits - 1 - b + log2(fine)) for b in range(bits)
    )
    d_col = to_col(d_row, p_rows)
    square = (p_rows, p_rows)
    earlier = jnp.logical_and(d_col == d_row, iota(square, 0) < iota(square, 1))
    rank_row = jnp.sum(jnp.where(earlier, 1.0, 0.0), axis=0, keepdims=True)
    slot_row = d_row * cap + rank_row
    for k in range(n_dp):
        slots = (iota((cap, p_rows), 0) + k * cap).astype(F32)
        sel[pl.ds(k * cap, cap), :] = jnp.where(slots == slot_row, 1.0, 0.0).astype(BF16)

    pl.semaphore_wait(barrier, n_dp + n_cent - 2)

    lab[at8(place), :] = jnp.broadcast_to(ca[...], (8, fine))
    for j in range(1, n_cent):
        mine = lab.at[at8(place)]
        go(mine, mine, lab_ss.at[j], lab_rs.at[j], z=cent_peer(j))
    def prepare(c):
        moved = jnp.dot(sel[...], points[:, pl.ds(starts[c], widths[c])], preferred_element_type=F32)
        send[c][...] = moved.astype(BF16)
        recv[c][span(me, cap), :] = send[c][span(me, cap), :]

    def dispatch(c):
        for j in range(1, n_dp):
            go(send[c].at[span(dp_peer(j), cap)], recv[c].at[span(me, cap)],
               a_ss.at[c, j], a_rs.at[c, j], d=dp_peer(j))

    prepare(0)
    dispatch(0)
    p_col = to_col(p_row.astype(F32), p_rows)
    rank_col = to_col(rank_row, p_rows)
    for k in range(n_dp):
        hit = jnp.where(d_col == k, rank_col, -1.0) == iota((p_rows, lanes), 1).astype(F32)
        row = jnp.sum(jnp.where(hit, p_col + 1.0, 0.0), axis=0, keepdims=True) - 1.0
        ids_s[pl.ds(k * 8, 8), :] = jnp.broadcast_to(row, (8, lanes))
    for j in range(1, n_dp):
        go(ids_s.at[at8(dp_peer(j))], ids_r.at[at8(me)], id_ss.at[j], id_rs.at[j], d=dp_peer(j))
    ids_r[at8(me), :] = ids_s[at8(me), :]
    for c in range(1, min(AHEAD, chunks)):
        prepare(c)
        dispatch(c)

    for j in range(1, n_cent):
        copy(lab.at[at8(place)], lab.at[at8(reverse(cent_peer(n_cent - j)))],
             lab_ss.at[j], lab_rs.at[j], z=cent_peer(n_cent - j)).wait_recv()
    small = (fine, fine)
    before = iota(small, 0) < iota(small, 1)
    labels = jnp.zeros((1, rows2), F32)
    pick = []
    for k in range(n_cent):
        row = lab[pl.ds(k * 8, 1), :]
        inside = jnp.where((row >> log2(block)) == mz, 1.0, 0.0)
        inside_col = to_col(inside, fine)
        value_col = to_col((row & (block - 1)).astype(F32), fine)
        rank = jnp.sum(jnp.where(before, inside_col, 0.0), axis=0, keepdims=True)
        slot = jnp.where(inside > 0.0, rank + k * cap2, -1.0)
        slot_col = to_col(slot, fine)
        hit = slot_col == iota((fine, rows2), 1).astype(F32)
        labels = labels + jnp.sum(jnp.where(hit, value_col + 1.0, 0.0), axis=0, keepdims=True)
        pick.append(jnp.where(slot == iota((rows2, fine), 0).astype(F32), 1.0, 0.0).astype(BF16))
    glab[at8(me), :] = jnp.broadcast_to(labels - 1.0, (8, rows2))
    for j in range(1, n_dp):
        mine = glab.at[at8(me)]
        go(mine, mine, gl_ss.at[j], gl_rs.at[j], d=dp_peer(j))

    for j in range(1, n_dp):
        copy(ids_s.at[at8(me)], ids_r.at[at8(dp_peer(n_dp - j))],
             id_ss.at[j], id_rs.at[j], d=dp_peer(n_dp - j)).wait_recv()
    tally = jnp.zeros((1, group), F32)
    for k in range(n_dp):
        row = ids_r[pl.ds(k * 8, 1), :]
        col = to_col(row, cap)
        part = jnp.where(col == iota((cap, group), 1).astype(F32), 1.0, 0.0)
        mt[pl.ds(k * cap, cap), :] = part.astype(BF16)
        tally = tally + jnp.sum(part, axis=0, keepdims=True)
        if cap % 128 == 0:
            hit = row == iota((group, cap), 0).astype(F32)
            m[:, pl.ds(k * cap, cap)] = jnp.where(hit, 1.0, 0.0).astype(BF16)
    for k in range(n_cent):
        cnt_s[pl.ds(k * 8, 8), :] = jnp.broadcast_to(tally[:, k * fine : (k + 1) * fine], (8, fine))
    for j in range(1, n_cent):
        go(cnt_s.at[at8(reverse(cent_peer(j)))], cnt_r.at[pl.ds(j * 8, 8)],
           cnt_ss.at[j], cnt_rs.at[j], z=cent_peer(j))

    acc[...] = jnp.zeros_like(acc)

    def fine_counts():
        for j in range(1, n_cent):
            copy(cnt_s.at[at8(place)], cnt_r.at[pl.ds(j * 8, 8)],
                 cnt_ss.at[j], cnt_rs.at[j], z=cent_peer(n_cent - j)).wait_recv()
        total = cnt_s[at8(place), :]
        for j in range(1, n_cent):
            total = total + cnt_r[pl.ds(j * 8, 8), :]
        fine_scale = jnp.maximum(to_col(total[0:1, :], fine), 1.0)
        return fine_scale

    def coarse_members():
        for j in range(1, n_dp):
            copy(glab.at[at8(me)], glab.at[at8(dp_peer(n_dp - j))],
                 gl_ss.at[j], gl_rs.at[j], d=dp_peer(n_dp - j)).wait_recv()
        coarse_tally = jnp.zeros((block, 1), F32)
        for k in range(n_dp):
            row = glab[pl.ds(k * 8, 1), :]
            part = jnp.where(row == iota((block, rows2), 0).astype(F32), 1.0, 0.0)
            g[:, pl.ds(k * rows2, rows2)] = part.astype(BF16)
            coarse_tally = coarse_tally + jnp.sum(part, axis=1, keepdims=True)
        coarse_scale = jnp.maximum(coarse_tally, 1.0)
        return coarse_scale

    def cent_partner(b):
        return mz + (1 - 2 * ((mz // (1 << b)) % 2)) * (1 << b)

    def keep(b):
        size = n_cent >> b
        return (place // size) * size

    def rs_parts(c, b):
        return (rs_out[b][c], rs_in[b][c], rs_ss.at[c, b], rs_rs.at[c, b])

    def rs_send(c, b):
        half = n_cent >> (b + 1)
        other = 2 * keep(b) + half - keep(b + 1)
        theirs = pl.ds(pl.multiple_of(other * fine, fine), half * fine)
        rs_out[b][c][...] = pf[c % live, theirs, : widths[c]].astype(BF16)
        go(*rs_parts(c, b), z=cent_partner(b))

    def rs_add(c, b):
        half = n_cent >> (b + 1)
        copy(*rs_parts(c, b), z=cent_partner(b)).wait_recv()
        mine = pl.ds(pl.multiple_of(keep(b + 1) * fine, fine), half * fine)
        pf[c % live, mine, : widths[c]] += rs_in[b][c][...].astype(F32)

    def ag_send(c):
        mine = cz[c].at[span(place, fine)]
        for j in range(1, n_cent):
            go(mine, mine, ag_ss.at[c, j], ag_rs.at[c, j], z=cent_peer(j))

    def ag_wait(c):
        for j in range(1, n_cent):
            source = cent_peer(n_cent - j)
            theirs = cz[c].at[span(reverse(source), fine)]
            copy(theirs, theirs, ag_ss.at[c, j], ag_rs.at[c, j], z=source).wait_recv()

    def sums(c):
        for j in range(1, n_dp):
            source = dp_peer(n_dp - j)
            copy(send[c].at[span(me, cap)], recv[c].at[span(source, cap)],
                 a_ss.at[c, j], a_rs.at[c, j], d=source).wait_recv()
        if c + AHEAD < chunks:
            prepare(c + AHEAD)
            dispatch(c + AHEAD)
        if cap % 128 == 0:
            pf[c % live, :, : widths[c]] = jnp.dot(m[...], recv[c][...], preferred_element_type=F32)
        else:
            pf[c % live, :, : widths[c]] = lax.dot_general(
                mt[...], recv[c][...], (((0,), (0,)), ((), ())), preferred_element_type=F32)
        rs_send(c, 0)

    def halve(b, c):
        rs_add(c, b - 1)
        rs_send(c, b)

    def centroids(c):
        rs_add(c, bits - 1)
        value = (pf[c % live, span(place, fine), : widths[c]] / fine_scale).astype(BF16)
        cz[c][span(place, fine), :] = value
        fine_out[:, pl.ds(starts[c], widths[c])] = value
        ag_send(c)

    def g_rows(c, d):
        return gr[c].at[span(d, rows2)]

    def g_args(c, k, d):
        return (g_rows(c, d), g_rows(c, d), g_ss.at[c, k], g_rs.at[c, k])

    if n_dp == 8:
        core = me % 2
        dx = (1 - 2 * ((me // 2) % 2)) * 2
        dy = (1 - 2 * ((me // 4) % 2)) * 4
        d1 = (1 - core) * dx + core * dy
        d2 = (1 - core) * dy + core * dx
        d3 = 1 - 2 * core

    def pick_rows(c):
        ag_wait(c)
        mine = jnp.dot(jnp.concatenate(pick, axis=1), cz[c][...], preferred_element_type=F32)
        gr[c][span(me, rows2), :] = mine.astype(BF16)
        if n_dp == 8:
            go(*g_args(c, 0, me), d=me + d1)
            go(*g_args(c, 1, me), d=me + d2)
            go(*g_args(c, 2, me), d=me + d3)
        else:
            for j in range(1, n_dp):
                go(*g_args(c, j, me), d=dp_peer(j))

    def spreads(c):
        near = jnp.dot(mt[...], cz[c][...], preferred_element_type=F32)
        gap = jnp.square(recv[c][...].astype(F32) - near)
        acc[...] += sum(gap[:, i : i + 128] for i in range(0, widths[c], 128))
        if c == chunks - 1:
            for k in range(n_dp):
                col = jnp.sum(acc[pl.ds(k * cap, cap), :], axis=1, keepdims=True) / width
                sp_s[pl.ds(k * 8, 8), :] = jnp.broadcast_to(to_row(col, lanes), (8, lanes))
            for j in range(1, n_dp):
                go(sp_s.at[at8(dp_peer(j))], sp_r.at[at8(me)], sp_ss.at[j], sp_rs.at[j], d=dp_peer(j))
            sp_r[at8(me), :] = sp_s[at8(me), :]

    def forward_one(c):
        if n_dp == 8:
            copy(*g_args(c, 0, me + d1), d=me + d1).wait_recv()
            go(*g_args(c, 3, me + d1), d=me + d2)
            go(*g_args(c, 4, me + d1), d=me + d3)
            copy(*g_args(c, 1, me + d2), d=me + d2).wait_recv()
            go(*g_args(c, 5, me + d2), d=me + d3)

    def forward_two(c):
        if n_dp == 8:
            copy(*g_args(c, 3, me + d1 + d2), d=me + d2).wait_recv()
            go(*g_args(c, 6, me + d1 + d2), d=me + d3)

    def finish(c):
        if n_dp == 8:
            copy(*g_args(c, 2, me + d3), d=me + d3).wait_recv()
            copy(*g_args(c, 4, me + d3 + d2), d=me + d3).wait_recv()
            copy(*g_args(c, 5, me + d3 + d1), d=me + d3).wait_recv()
            copy(*g_args(c, 6, me + d3 + d1 + d2), d=me + d3).wait_recv()
        else:
            for j in range(1, n_dp):
                source = dp_peer(n_dp - j)
                copy(*g_args(c, j, source), d=source).wait_recv()
        result = jnp.dot(g[...], gr[c][...], preferred_element_type=F32)
        coarse_out[:, pl.ds(starts[c], widths[c])] = (result / coarse_scale).astype(BF16)

    stages = [sums]
    stages += [functools.partial(halve, b) for b in range(1, bits)]
    stages += [centroids]
    stages += [pick_rows, forward_one, forward_two]
    late = [(len(stages) - 3, spreads), (len(stages), finish)]
    for tick in range(chunks + len(stages)):
        for s in reversed(range(len(stages))):
            if 0 <= tick - s < chunks:
                stages[s](tick - s)
        if tick == 0:
            fine_scale = fine_counts()
        if tick == 1:
            coarse_scale = coarse_members()
        for s, stage in late:
            if 0 <= tick - s < chunks:
                stage(tick - s)

    for j in range(1, n_dp):
        source = dp_peer(n_dp - j)
        copy(sp_s.at[at8(me)], sp_r.at[at8(source)], sp_ss.at[j], sp_rs.at[j], d=source).wait_recv()
    spread = jnp.zeros((1, p_rows), F32)
    for k in range(n_dp):
        col = to_col(sp_r[pl.ds(k * 8, 1), :], cap)
        slots = (iota((cap, p_rows), 0) + k * cap).astype(F32)
        spread = spread + jnp.sum(jnp.where(slots == slot_row, col, 0.0), axis=0, keepdims=True)
    spread_out[...] = spread
    for made in started:
        made.wait_send()


def place_results(*refs):
    n = 3
    ins, outs, held, (sem_in, sem_out) = refs[:n], refs[n : 2 * n], refs[2 * n : 3 * n], refs[3 * n :]
    parts = []
    for i in (2, 1, 0):
        count = PARTS if i == 2 else 1
        rows = ins[i].shape[0] // count
        parts += [(i, pl.ds(k * rows, rows)) for k in range(count)]
    first = [
        pltpu.make_async_copy(ins[i].at[at], held[i].at[at], sem_in.at[k])
        for k, (i, at) in enumerate(parts)
    ]
    second = [
        pltpu.make_async_copy(held[i].at[at], outs[i].at[at], sem_out.at[k])
        for k, (i, at) in enumerate(parts)
    ]
    for move in first:
        move.start()
    for k, move in enumerate(first):
        move.wait()
        second[k].start()
    for move in second:
        move.wait()


def body(points, fine_assign, coarse_assign):
    n_dp = lax.axis_size("dp")
    n_cent = lax.axis_size("cent")
    p_rows, width = points.shape
    fine = coarse_assign.shape[0]
    sources = n_dp * n_cent
    cap = max(2, 2 * p_rows // sources) * n_cent
    cap2 = max(2, 2 * fine // n_cent)
    block = COARSE // n_cent
    parts = (1, 2, 2, 2, 1) if n_cent == 4 else (1,) * 8
    widths = tuple(width // 8 * part for part in parts)
    chunks = len(widths)
    bits = log2(n_cent)
    group, slots, rows2, lanes = n_cent * fine, n_dp * cap, n_cent * cap2, max(cap, 128)
    cfg = (n_dp, n_cent, p_rows, fine, width, widths, cap, cap2, block)
    half_rows = [(n_cent >> (b + 1)) * fine for b in range(bits)]
    heights = [slots, slots, group, n_dp * rows2, *half_rows, *half_rows]
    dma = pltpu.SemaphoreType.DMA
    scratch = [
        pltpu.VMEM((slots, p_rows), BF16),
        pltpu.VMEM((slots, group), BF16),
        pltpu.VMEM((group, slots) if cap % 128 == 0 else (16, 128), BF16),
        pltpu.VMEM((bits + 1, group, max(widths)), F32),
        pltpu.VMEM((block, n_dp * rows2), BF16),
        pltpu.VMEM((n_dp * 8, lanes), F32),
        pltpu.VMEM((n_dp * 8, lanes), F32),
        pltpu.VMEM((n_cent * 8, fine), I32),
        pltpu.VMEM((n_dp * 8, rows2), F32),
        pltpu.VMEM((n_cent * 8, fine), F32),
        pltpu.VMEM((n_cent * 8, fine), F32),
        pltpu.VMEM((n_dp * 8, lanes), F32),
        pltpu.VMEM((n_dp * 8, lanes), F32),
        pltpu.VMEM((slots, 128), F32),
        *(pltpu.VMEM((height, w), BF16) for height in heights for w in widths),
        dma((chunks, n_dp)), dma((chunks, n_dp)),
        dma((chunks, bits)), dma((chunks, bits)),
        dma((chunks, n_cent)), dma((chunks, n_cent)),
        dma((chunks, n_dp)), dma((chunks, n_dp)),
        dma((n_dp,)), dma((n_dp,)),
        dma((n_cent,)), dma((n_cent,)),
        dma((n_cent,)), dma((n_cent,)),
        dma((n_dp,)), dma((n_dp,)),
        dma((n_dp,)), dma((n_dp,)),
    ]
    vmem = pl.BlockSpec(memory_space=pltpu.VMEM)
    results = pl.pallas_call(
        functools.partial(kernel, cfg),
        out_shape=(
            jax.ShapeDtypeStruct((1, p_rows), F32),
            jax.ShapeDtypeStruct((fine, width), BF16),
            jax.ShapeDtypeStruct((block, width), BF16),
        ),
        in_specs=[vmem] * 3,
        out_specs=(vmem,) * 3,
        scratch_shapes=scratch,
        compiler_params=pltpu.CompilerParams(
            collective_id=0, has_side_effects=True, vmem_limit_bytes=60 * 1024 * 1024
        ),
        cost_estimate=pl.CostEstimate(
            flops=2 * width * (slots * (p_rows + 2 * group) + block * n_dp * rows2),
            bytes_accessed=2 * width * (p_rows + fine + block),
            transcendentals=0,
        ),
    )(points, fine_assign.reshape(1, p_rows), coarse_assign.reshape(1, fine))
    anywhere = pl.BlockSpec(memory_space=pl.ANY)
    spread, fine_centroids, coarse_centroids = pl.pallas_call(
        place_results,
        out_shape=tuple(jax.ShapeDtypeStruct(r.shape, r.dtype) for r in results),
        in_specs=[anywhere] * 3,
        out_specs=(anywhere,) * 3,
        scratch_shapes=[
            *(pltpu.VMEM(r.shape, r.dtype) for r in results),
            dma((PARTS + 2,)),
            dma((PARTS + 2,)),
        ],
    )(*results)
    return (spread.reshape(p_rows), fine_centroids, coarse_centroids)


def solution(mesh):
    placed = (P(("dp", "cent"), None), P(("dp", "cent")), P(("dp", "cent")))
    return jax.shard_map(
        body,
        mesh=mesh,
        in_specs=placed,
        out_specs=(P(("dp", "cent")), P(("dp", "cent"), None), P("cent", None)),
        check_vma=False,
    )
```

```python
import functools

import jax
import jax.numpy as jnp
from jax import lax
from jax.experimental import pallas as pl
from jax.experimental.pallas import tpu as pltpu
from jax.sharding import PartitionSpec as P

COARSE = 4096
AHEAD = 3
PARTS = 4
MESH = pl.DeviceIdType.MESH
F32 = jnp.float32
BF16 = jnp.bfloat16
I32 = jnp.int32


def log2(n):
    assert n & (n - 1) == 0
    return n.bit_length() - 1


def iota(shape, dim):
    return lax.broadcasted_iota(I32, shape, dim)


def to_col(row, rows):
    shape = (rows, row.shape[1])
    same = iota(shape, 0) == iota(shape, 1)
    return jnp.sum(jnp.where(same, row, 0.0), axis=1, keepdims=True)


def to_row(col, lanes):
    shape = (col.shape[0], lanes)
    same = iota(shape, 0) == iota(shape, 1)
    return jnp.sum(jnp.where(same, col, 0.0), axis=0, keepdims=True)


def kernel(cfg, *refs):
    (n_dp, n_cent, p_rows, fine, width, widths, cap, cap2, block) = cfg
    (points, fa, ca, spread_out, fine_out, coarse_out,
     sel, mt, m, pf, g,
     ids_s, ids_r, lab, glab, cnt_s, cnt_r, sp_s, sp_r, acc) = refs[:20]
    bits = log2(n_cent)
    chunks = len(widths)
    starts = [sum(widths[:c]) for c in range(chunks)]
    lists = [refs[20 + k * chunks : 20 + (k + 1) * chunks] for k in range(4 + 2 * bits)]
    send, recv, cz, gr = lists[:4]
    rs_out, rs_in = lists[4 : 4 + bits], lists[4 + bits :]
    (a_ss, a_rs, rs_ss, rs_rs, ag_ss, ag_rs, g_ss, g_rs,
     id_ss, id_rs, lab_ss, lab_rs, cnt_ss, cnt_rs, gl_ss, gl_rs, sp_ss, sp_rs) = refs[20 + (4 + 2 * bits) * chunks :]
    group = n_cent * fine
    live = bits + 1
    rows2 = n_cent * cap2
    lanes = max(cap, 128)
    me = lax.axis_index("dp")
    mz = lax.axis_index("cent")

    def reverse(z):
        return sum(((z // (1 << b)) % 2) * (1 << (bits - 1 - b)) for b in range(bits))

    place = reverse(mz)

    def at8(k):
        return pl.ds(pl.multiple_of(k * 8, 8), 8)

    def span(k, size):
        return pl.ds(pl.multiple_of(k * size, size), size)

    def dp_peer(j):
        return lax.rem(me + j, n_dp)

    def cent_peer(j):
        return lax.rem(mz + j, n_cent)

    started = []

    def copy(src, dst, ss, rs, d=None, z=None):
        made = pltpu.make_async_remote_copy(
            src_ref=src, dst_ref=dst, send_sem=ss, recv_sem=rs,
            device_id=(me if d is None else d, mz if z is None else z), device_id_type=MESH,
        )
        return made

    def go(*args, **kwargs):
        made = copy(*args, **kwargs)
        made.start()
        started.append(made)
        return made

    barrier = pltpu.get_barrier_semaphore()
    for j in range(1, n_dp):
        pl.semaphore_signal(barrier, inc=1, device_id=(dp_peer(j), mz), device_id_type=MESH)
    for j in range(1, n_cent):
        pl.semaphore_signal(barrier, inc=1, device_id=(me, cent_peer(j)), device_id_type=MESH)

    f_row = fa[...]
    d_row = (f_row >> log2(group)).astype(F32)
    z_row = (f_row & (group - 1)) >> log2(fine)
    p_row = (f_row & (fine - 1)) + sum(
        ((z_row >> b) & 1) << (bits - 1 - b + log2(fine)) for b in range(bits)
    )
    d_col = to_col(d_row, p_rows)
    square = (p_rows, p_rows)
    earlier = jnp.logical_and(d_col == d_row, iota(square, 0) < iota(square, 1))
    rank_row = jnp.sum(jnp.where(earlier, 1.0, 0.0), axis=0, keepdims=True)
    slot_row = d_row * cap + rank_row
    for k in range(n_dp):
        slots = (iota((cap, p_rows), 0) + k * cap).astype(F32)
        sel[pl.ds(k * cap, cap), :] = jnp.where(slots == slot_row, 1.0, 0.0).astype(BF16)

    pl.semaphore_wait(barrier, n_dp + n_cent - 2)

    lab[at8(place), :] = jnp.broadcast_to(ca[...], (8, fine))
    for j in range(1, n_cent):
        mine = lab.at[at8(place)]
        go(mine, mine, lab_ss.at[j], lab_rs.at[j], z=cent_peer(j))
    def prepare(c):
        moved = jnp.dot(sel[...], points[:, pl.ds(starts[c], widths[c])], preferred_element_type=F32)
        send[c][...] = moved.astype(BF16)
        recv[c][span(me, cap), :] = send[c][span(me, cap), :]

    def dispatch(c):
        for j in range(1, n_dp):
            go(send[c].at[span(dp_peer(j), cap)], recv[c].at[span(me, cap)],
               a_ss.at[c, j], a_rs.at[c, j], d=dp_peer(j))

    prepare(0)
    dispatch(0)
    p_col = to_col(p_row.astype(F32), p_rows)
    rank_col = to_col(rank_row, p_rows)
    for k in range(n_dp):
        hit = jnp.where(d_col == k, rank_col, -1.0) == iota((p_rows, lanes), 1).astype(F32)
        row = jnp.sum(jnp.where(hit, p_col + 1.0, 0.0), axis=0, keepdims=True) - 1.0
        ids_s[pl.ds(k * 8, 8), :] = jnp.broadcast_to(row, (8, lanes))
    for j in range(1, n_dp):
        go(ids_s.at[at8(dp_peer(j))], ids_r.at[at8(me)], id_ss.at[j], id_rs.at[j], d=dp_peer(j))
    ids_r[at8(me), :] = ids_s[at8(me), :]
    for c in range(1, min(AHEAD, chunks)):
        prepare(c)
        dispatch(c)

    for j in range(1, n_cent):
        copy(lab.at[at8(place)], lab.at[at8(reverse(cent_peer(n_cent - j)))],
             lab_ss.at[j], lab_rs.at[j], z=cent_peer(n_cent - j)).wait_recv()
    small = (fine, fine)
    before = iota(small, 0) < iota(small, 1)
    labels = jnp.zeros((1, rows2), F32)
    pick = []
    for k in range(n_cent):
        row = lab[pl.ds(k * 8, 1), :]
        inside = jnp.where((row >> log2(block)) == mz, 1.0, 0.0)
        inside_col = to_col(inside, fine)
        value_col = to_col((row & (block - 1)).astype(F32), fine)
        rank = jnp.sum(jnp.where(before, inside_col, 0.0), axis=0, keepdims=True)
        slot = jnp.where(inside > 0.0, rank + k * cap2, -1.0)
        slot_col = to_col(slot, fine)
        hit = slot_col == iota((fine, rows2), 1).astype(F32)
        labels = labels + jnp.sum(jnp.where(hit, value_col + 1.0, 0.0), axis=0, keepdims=True)
        pick.append(jnp.where(slot == iota((rows2, fine), 0).astype(F32), 1.0, 0.0).astype(BF16))
    glab[at8(me), :] = jnp.broadcast_to(labels - 1.0, (8, rows2))
    for j in range(1, n_dp):
        mine = glab.at[at8(me)]
        go(mine, mine, gl_ss.at[j], gl_rs.at[j], d=dp_peer(j))

    for j in range(1, n_dp):
        copy(ids_s.at[at8(me)], ids_r.at[at8(dp_peer(n_dp - j))],
             id_ss.at[j], id_rs.at[j], d=dp_peer(n_dp - j)).wait_recv()
    tally = jnp.zeros((1, group), F32)
    for k in range(n_dp):
        row = ids_r[pl.ds(k * 8, 1), :]
        col = to_col(row, cap)
        part = jnp.where(col == iota((cap, group), 1).astype(F32), 1.0, 0.0)
        mt[pl.ds(k * cap, cap), :] = part.astype(BF16)
        tally = tally + jnp.sum(part, axis=0, keepdims=True)
        if cap % 128 == 0:
            hit = row == iota((group, cap), 0).astype(F32)
            m[:, pl.ds(k * cap, cap)] = jnp.where(hit, 1.0, 0.0).astype(BF16)
    for k in range(n_cent):
        cnt_s[pl.ds(k * 8, 8), :] = jnp.broadcast_to(tally[:, k * fine : (k + 1) * fine], (8, fine))
    for j in range(1, n_cent):
        go(cnt_s.at[at8(reverse(cent_peer(j)))], cnt_r.at[pl.ds(j * 8, 8)],
           cnt_ss.at[j], cnt_rs.at[j], z=cent_peer(j))

    acc[...] = jnp.zeros_like(acc)

    def fine_counts():
        for j in range(1, n_cent):
            copy(cnt_s.at[at8(place)], cnt_r.at[pl.ds(j * 8, 8)],
                 cnt_ss.at[j], cnt_rs.at[j], z=cent_peer(n_cent - j)).wait_recv()
        total = cnt_s[at8(place), :]
        for j in range(1, n_cent):
            total = total + cnt_r[pl.ds(j * 8, 8), :]
        fine_scale = jnp.maximum(to_col(total[0:1, :], fine), 1.0)
        return fine_scale

    def coarse_members():
        for j in range(1, n_dp):
            copy(glab.at[at8(me)], glab.at[at8(dp_peer(n_dp - j))],
                 gl_ss.at[j], gl_rs.at[j], d=dp_peer(n_dp - j)).wait_recv()
        coarse_tally = jnp.zeros((block, 1), F32)
        for k in range(n_dp):
            row = glab[pl.ds(k * 8, 1), :]
            part = jnp.where(row == iota((block, rows2), 0).astype(F32), 1.0, 0.0)
            g[:, pl.ds(k * rows2, rows2)] = part.astype(BF16)
            coarse_tally = coarse_tally + jnp.sum(part, axis=1, keepdims=True)
        coarse_scale = jnp.maximum(coarse_tally, 1.0)
        return coarse_scale

    def cent_partner(b):
        return mz + (1 - 2 * ((mz // (1 << b)) % 2)) * (1 << b)

    def keep(b):
        size = n_cent >> b
        return (place // size) * size

    def rs_parts(c, b):
        return (rs_out[b][c], rs_in[b][c], rs_ss.at[c, b], rs_rs.at[c, b])

    def rs_send(c, b):
        half = n_cent >> (b + 1)
        other = 2 * keep(b) + half - keep(b + 1)
        theirs = pl.ds(pl.multiple_of(other * fine, fine), half * fine)
        rs_out[b][c][...] = pf[c % live, theirs, : widths[c]].astype(BF16)
        go(*rs_parts(c, b), z=cent_partner(b))

    def rs_add(c, b):
        half = n_cent >> (b + 1)
        copy(*rs_parts(c, b), z=cent_partner(b)).wait_recv()
        mine = pl.ds(pl.multiple_of(keep(b + 1) * fine, fine), half * fine)
        pf[c % live, mine, : widths[c]] += rs_in[b][c][...].astype(F32)

    def ag_send(c):
        mine = cz[c].at[span(place, fine)]
        for j in range(1, n_cent):
            go(mine, mine, ag_ss.at[c, j], ag_rs.at[c, j], z=cent_peer(j))

    def ag_wait(c):
        for j in range(1, n_cent):
            source = cent_peer(n_cent - j)
            theirs = cz[c].at[span(reverse(source), fine)]
            copy(theirs, theirs, ag_ss.at[c, j], ag_rs.at[c, j], z=source).wait_recv()

    def sums(c):
        for j in range(1, n_dp):
            source = dp_peer(n_dp - j)
            copy(send[c].at[span(me, cap)], recv[c].at[span(source, cap)],
                 a_ss.at[c, j], a_rs.at[c, j], d=source).wait_recv()
        if c + AHEAD < chunks:
            prepare(c + AHEAD)
            dispatch(c + AHEAD)
        if cap % 128 == 0:
            pf[c % live, :, : widths[c]] = jnp.dot(m[...], recv[c][...], preferred_element_type=F32)
        else:
            pf[c % live, :, : widths[c]] = lax.dot_general(
                mt[...], recv[c][...], (((0,), (0,)), ((), ())), preferred_element_type=F32)
        rs_send(c, 0)

    def halve(b, c):
        rs_add(c, b - 1)
        rs_send(c, b)

    def centroids(c):
        rs_add(c, bits - 1)
        value = (pf[c % live, span(place, fine), : widths[c]] / fine_scale).astype(BF16)
        cz[c][span(place, fine), :] = value
        fine_out[:, pl.ds(starts[c], widths[c])] = value
        ag_send(c)

    def g_rows(c, d):
        return gr[c].at[span(d, rows2)]

    def g_args(c, k, d):
        return (g_rows(c, d), g_rows(c, d), g_ss.at[c, k], g_rs.at[c, k])

    if n_dp == 8:
        core = me % 2
        dx = (1 - 2 * ((me // 2) % 2)) * 2
        dy = (1 - 2 * ((me // 4) % 2)) * 4
        d1 = (1 - core) * dx + core * dy
        d2 = (1 - core) * dy + core * dx
        d3 = 1 - 2 * core

    def pick_rows(c):
        ag_wait(c)
        mine = jnp.dot(jnp.concatenate(pick, axis=1), cz[c][...], preferred_element_type=F32)
        gr[c][span(me, rows2), :] = mine.astype(BF16)
        if n_dp == 8:
            go(*g_args(c, 0, me), d=me + d1)
            go(*g_args(c, 1, me), d=me + d2)
            go(*g_args(c, 2, me), d=me + d3)
        else:
            for j in range(1, n_dp):
                go(*g_args(c, j, me), d=dp_peer(j))

    def spreads(c):
        near = jnp.dot(mt[...], cz[c][...], preferred_element_type=F32)
        gap = jnp.square(recv[c][...].astype(F32) - near)
        acc[...] += sum(gap[:, i : i + 128] for i in range(0, widths[c], 128))
        if c == chunks - 1:
            for k in range(n_dp):
                col = jnp.sum(acc[pl.ds(k * cap, cap), :], axis=1, keepdims=True) / width
                sp_s[pl.ds(k * 8, 8), :] = jnp.broadcast_to(to_row(col, lanes), (8, lanes))
            for j in range(1, n_dp):
                go(sp_s.at[at8(dp_peer(j))], sp_r.at[at8(me)], sp_ss.at[j], sp_rs.at[j], d=dp_peer(j))
            sp_r[at8(me), :] = sp_s[at8(me), :]

    def forward_one(c):
        if n_dp == 8:
            copy(*g_args(c, 0, me + d1), d=me + d1).wait_recv()
            go(*g_args(c, 3, me + d1), d=me + d2)
            go(*g_args(c, 4, me + d1), d=me + d3)
            copy(*g_args(c, 1, me + d2), d=me + d2).wait_recv()
            go(*g_args(c, 5, me + d2), d=me + d3)

    def forward_two(c):
        if n_dp == 8:
            copy(*g_args(c, 3, me + d1 + d2), d=me + d2).wait_recv()
            go(*g_args(c, 6, me + d1 + d2), d=me + d3)

    def finish(c):
        if n_dp == 8:
            copy(*g_args(c, 2, me + d3), d=me + d3).wait_recv()
            copy(*g_args(c, 4, me + d3 + d2), d=me + d3).wait_recv()
            copy(*g_args(c, 5, me + d3 + d1), d=me + d3).wait_recv()
            copy(*g_args(c, 6, me + d3 + d1 + d2), d=me + d3).wait_recv()
        else:
            for j in range(1, n_dp):
                source = dp_peer(n_dp - j)
                copy(*g_args(c, j, source), d=source).wait_recv()
        result = jnp.dot(g[...], gr[c][...], preferred_element_type=F32)
        coarse_out[:, pl.ds(starts[c], widths[c])] = (result / coarse_scale).astype(BF16)

    stages = [sums]
    stages += [functools.partial(halve, b) for b in range(1, bits)]
    stages += [centroids]
    stages += [pick_rows, forward_one, forward_two]
    late = [(len(stages) - 3, spreads), (len(stages), finish)]
    for tick in range(chunks + len(stages)):
        for s in reversed(range(len(stages))):
            if 0 <= tick - s < chunks:
                stages[s](tick - s)
        if tick == 0:
            fine_scale = fine_counts()
        if tick == 1:
            coarse_scale = coarse_members()
        for s, stage in late:
            if 0 <= tick - s < chunks:
                stage(tick - s)

    for j in range(1, n_dp):
        source = dp_peer(n_dp - j)
        copy(sp_s.at[at8(me)], sp_r.at[at8(source)], sp_ss.at[j], sp_rs.at[j], d=source).wait_recv()
    spread = jnp.zeros((1, p_rows), F32)
    for k in range(n_dp):
        col = to_col(sp_r[pl.ds(k * 8, 1), :], cap)
        slots = (iota((cap, p_rows), 0) + k * cap).astype(F32)
        spread = spread + jnp.sum(jnp.where(slots == slot_row, col, 0.0), axis=0, keepdims=True)
    spread_out[...] = spread
    for made in started:
        made.wait_send()


def place_results(*refs):
    n = 3
    ins, outs, held, (sem_in, sem_out) = refs[:n], refs[n : 2 * n], refs[2 * n : 3 * n], refs[3 * n :]
    parts = []
    for i in (2, 1, 0):
        count = PARTS if i == 2 else 1
        rows = ins[i].shape[0] // count
        parts += [(i, pl.ds(k * rows, rows)) for k in range(count)]
    first = [
        pltpu.make_async_copy(ins[i].at[at], held[i].at[at], sem_in.at[k])
        for k, (i, at) in enumerate(parts)
    ]
    second = [
        pltpu.make_async_copy(held[i].at[at], outs[i].at[at], sem_out.at[k])
        for k, (i, at) in enumerate(parts)
    ]
    for move in first:
        move.start()
    for k, move in enumerate(first):
        move.wait()
        second[k].start()
    for move in second:
        move.wait()


def body(points, fine_assign, coarse_assign):
    n_dp = lax.axis_size("dp")
    n_cent = lax.axis_size("cent")
    p_rows, width = points.shape
    fine = coarse_assign.shape[0]
    sources = n_dp * n_cent
    cap = max(2, 2 * p_rows // sources) * n_cent
    cap2 = max(2, 2 * fine // n_cent)
    block = COARSE // n_cent
    parts = (1,) * 8
    widths = tuple(width // 8 * part for part in parts)
    chunks = len(widths)
    bits = log2(n_cent)
    group, slots, rows2, lanes = n_cent * fine, n_dp * cap, n_cent * cap2, max(cap, 128)
    cfg = (n_dp, n_cent, p_rows, fine, width, widths, cap, cap2, block)
    half_rows = [(n_cent >> (b + 1)) * fine for b in range(bits)]
    heights = [slots, slots, group, n_dp * rows2, *half_rows, *half_rows]
    dma = pltpu.SemaphoreType.DMA
    scratch = [
        pltpu.VMEM((slots, p_rows), BF16),
        pltpu.VMEM((slots, group), BF16),
        pltpu.VMEM((group, slots) if cap % 128 == 0 else (16, 128), BF16),
        pltpu.VMEM((bits + 1, group, max(widths)), F32),
        pltpu.VMEM((block, n_dp * rows2), BF16),
        pltpu.VMEM((n_dp * 8, lanes), F32),
        pltpu.VMEM((n_dp * 8, lanes), F32),
        pltpu.VMEM((n_cent * 8, fine), I32),
        pltpu.VMEM((n_dp * 8, rows2), F32),
        pltpu.VMEM((n_cent * 8, fine), F32),
        pltpu.VMEM((n_cent * 8, fine), F32),
        pltpu.VMEM((n_dp * 8, lanes), F32),
        pltpu.VMEM((n_dp * 8, lanes), F32),
        pltpu.VMEM((slots, 128), F32),
        *(pltpu.VMEM((height, w), BF16) for height in heights for w in widths),
        dma((chunks, n_dp)), dma((chunks, n_dp)),
        dma((chunks, bits)), dma((chunks, bits)),
        dma((chunks, n_cent)), dma((chunks, n_cent)),
        dma((chunks, n_dp)), dma((chunks, n_dp)),
        dma((n_dp,)), dma((n_dp,)),
        dma((n_cent,)), dma((n_cent,)),
        dma((n_cent,)), dma((n_cent,)),
        dma((n_dp,)), dma((n_dp,)),
        dma((n_dp,)), dma((n_dp,)),
    ]
    vmem = pl.BlockSpec(memory_space=pltpu.VMEM)
    results = pl.pallas_call(
        functools.partial(kernel, cfg),
        out_shape=(
            jax.ShapeDtypeStruct((1, p_rows), F32),
            jax.ShapeDtypeStruct((fine, width), BF16),
            jax.ShapeDtypeStruct((block, width), BF16),
        ),
        in_specs=[vmem] * 3,
        out_specs=(vmem,) * 3,
        scratch_shapes=scratch,
        compiler_params=pltpu.CompilerParams(
            collective_id=0, has_side_effects=True, vmem_limit_bytes=60 * 1024 * 1024
        ),
        cost_estimate=pl.CostEstimate(
            flops=2 * width * (slots * (p_rows + 2 * group) + block * n_dp * rows2),
            bytes_accessed=2 * width * (p_rows + fine + block),
            transcendentals=0,
        ),
    )(points, fine_assign.reshape(1, p_rows), coarse_assign.reshape(1, fine))
    anywhere = pl.BlockSpec(memory_space=pl.ANY)
    spread, fine_centroids, coarse_centroids = pl.pallas_call(
        place_results,
        out_shape=tuple(jax.ShapeDtypeStruct(r.shape, r.dtype) for r in results),
        in_specs=[anywhere] * 3,
        out_specs=(anywhere,) * 3,
        scratch_shapes=[
            *(pltpu.VMEM(r.shape, r.dtype) for r in results),
            dma((PARTS + 2,)),
            dma((PARTS + 2,)),
        ],
    )(*results)
    return (spread.reshape(p_rows), fine_centroids, coarse_centroids)


def solution(mesh):
    placed = (P(("dp", "cent"), None), P(("dp", "cent")), P(("dp", "cent")))
    return jax.shard_map(
        body,
        mesh=mesh,
        in_specs=placed,
        out_specs=(P(("dp", "cent")), P(("dp", "cent"), None), P("cent", None)),
        check_vma=False,
    )
```

```python
import functools

import jax
import jax.numpy as jnp
from jax import lax
from jax.experimental import pallas as pl
from jax.experimental.pallas import tpu as pltpu
from jax.sharding import PartitionSpec as P

COARSE = 4096
CHUNKS = 8
AHEAD = 2
PARTS = 4
MESH = pl.DeviceIdType.MESH
F32 = jnp.float32
BF16 = jnp.bfloat16
I32 = jnp.int32


def log2(n):
    assert n & (n - 1) == 0
    return n.bit_length() - 1


def iota(shape, dim):
    return lax.broadcasted_iota(I32, shape, dim)


def to_col(row, rows):
    shape = (rows, row.shape[1])
    same = iota(shape, 0) == iota(shape, 1)
    return jnp.sum(jnp.where(same, row, 0.0), axis=1, keepdims=True)


def to_row(col, lanes):
    shape = (col.shape[0], lanes)
    same = iota(shape, 0) == iota(shape, 1)
    return jnp.sum(jnp.where(same, col, 0.0), axis=0, keepdims=True)


def kernel(cfg, *refs):
    (n_dp, n_cent, p_rows, fine, width, w, cap, cap2, block) = cfg
    (points, fa, ca, spread_out, fine_out, coarse_out,
     sel, send, recv, mt, m, pf, cz, gr, g,
     ids_s, ids_r, lab, glab, cnt_s, cnt_r, sp_s, sp_r, acc) = refs[:24]
    bits = log2(n_cent)
    rs_out = refs[24 : 24 + bits]
    rs_in = refs[24 + bits : 24 + 2 * bits]
    (a_ss, a_rs, rs_ss, rs_rs, ag_ss, ag_rs, g_ss, g_rs,
     id_ss, id_rs, lab_ss, lab_rs, cnt_ss, cnt_rs, gl_ss, gl_rs, sp_ss, sp_rs) = refs[24 + 2 * bits :]
    chunks = width // w
    group = n_cent * fine
    live = bits + 1
    rows2 = n_cent * cap2
    lanes = max(cap, 128)
    me = lax.axis_index("dp")
    mz = lax.axis_index("cent")

    def reverse(z):
        return sum(((z // (1 << b)) % 2) * (1 << (bits - 1 - b)) for b in range(bits))

    place = reverse(mz)

    def at8(k):
        return pl.ds(pl.multiple_of(k * 8, 8), 8)

    def span(k, size):
        return pl.ds(pl.multiple_of(k * size, size), size)

    def dp_peer(j):
        return lax.rem(me + j, n_dp)

    def cent_peer(j):
        return lax.rem(mz + j, n_cent)

    started = []

    def copy(src, dst, ss, rs, d=None, z=None):
        made = pltpu.make_async_remote_copy(
            src_ref=src, dst_ref=dst, send_sem=ss, recv_sem=rs,
            device_id=(me if d is None else d, mz if z is None else z), device_id_type=MESH,
        )
        return made

    def go(*args, **kwargs):
        made = copy(*args, **kwargs)
        made.start()
        started.append(made)
        return made

    barrier = pltpu.get_barrier_semaphore()
    for j in range(1, n_dp):
        pl.semaphore_signal(barrier, inc=1, device_id=(dp_peer(j), mz), device_id_type=MESH)
    for j in range(1, n_cent):
        pl.semaphore_signal(barrier, inc=1, device_id=(me, cent_peer(j)), device_id_type=MESH)

    f_row = fa[...]
    d_row = (f_row >> log2(group)).astype(F32)
    z_row = (f_row & (group - 1)) >> log2(fine)
    p_row = (f_row & (fine - 1)) + sum(
        ((z_row >> b) & 1) << (bits - 1 - b + log2(fine)) for b in range(bits)
    )
    d_col = to_col(d_row, p_rows)
    square = (p_rows, p_rows)
    earlier = jnp.logical_and(d_col == d_row, iota(square, 0) < iota(square, 1))
    rank_row = jnp.sum(jnp.where(earlier, 1.0, 0.0), axis=0, keepdims=True)
    slot_row = d_row * cap + rank_row
    for k in range(n_dp):
        slots = (iota((cap, p_rows), 0) + k * cap).astype(F32)
        sel[pl.ds(k * cap, cap), :] = jnp.where(slots == slot_row, 1.0, 0.0).astype(BF16)

    pl.semaphore_wait(barrier, n_dp + n_cent - 2)

    lab[at8(place), :] = jnp.broadcast_to(ca[...], (8, fine))
    for j in range(1, n_cent):
        mine = lab.at[at8(place)]
        go(mine, mine, lab_ss.at[j], lab_rs.at[j], z=cent_peer(j))
    def prepare(c):
        moved = jnp.dot(sel[...], points[:, pl.ds(c * w, w)], preferred_element_type=F32)
        send[c] = moved.astype(BF16)
        recv[c, span(me, cap), :] = send[c, span(me, cap), :]

    def dispatch(c):
        for j in range(1, n_dp):
            go(send.at[c, span(dp_peer(j), cap)], recv.at[c, span(me, cap)],
               a_ss.at[c, j], a_rs.at[c, j], d=dp_peer(j))

    prepare(0)
    dispatch(0)
    p_col = to_col(p_row.astype(F32), p_rows)
    rank_col = to_col(rank_row, p_rows)
    for k in range(n_dp):
        hit = jnp.where(d_col == k, rank_col, -1.0) == iota((p_rows, lanes), 1).astype(F32)
        row = jnp.sum(jnp.where(hit, p_col + 1.0, 0.0), axis=0, keepdims=True) - 1.0
        ids_s[pl.ds(k * 8, 8), :] = jnp.broadcast_to(row, (8, lanes))
    for j in range(1, n_dp):
        go(ids_s.at[at8(dp_peer(j))], ids_r.at[at8(me)], id_ss.at[j], id_rs.at[j], d=dp_peer(j))
    ids_r[at8(me), :] = ids_s[at8(me), :]
    for c in range(1, chunks):
        prepare(c)
        if c < AHEAD:
            dispatch(c)

    for j in range(1, n_cent):
        copy(lab.at[at8(place)], lab.at[at8(reverse(cent_peer(n_cent - j)))],
             lab_ss.at[j], lab_rs.at[j], z=cent_peer(n_cent - j)).wait_recv()
    small = (fine, fine)
    before = iota(small, 0) < iota(small, 1)
    labels = jnp.zeros((1, rows2), F32)
    pick = []
    for k in range(n_cent):
        row = lab[pl.ds(k * 8, 1), :]
        inside = jnp.where((row >> log2(block)) == mz, 1.0, 0.0)
        inside_col = to_col(inside, fine)
        value_col = to_col((row & (block - 1)).astype(F32), fine)
        rank = jnp.sum(jnp.where(before, inside_col, 0.0), axis=0, keepdims=True)
        slot = jnp.where(inside > 0.0, rank + k * cap2, -1.0)
        slot_col = to_col(slot, fine)
        hit = slot_col == iota((fine, rows2), 1).astype(F32)
        labels = labels + jnp.sum(jnp.where(hit, value_col + 1.0, 0.0), axis=0, keepdims=True)
        pick.append(jnp.where(slot == iota((rows2, fine), 0).astype(F32), 1.0, 0.0).astype(BF16))
    glab[at8(me), :] = jnp.broadcast_to(labels - 1.0, (8, rows2))
    for j in range(1, n_dp):
        mine = glab.at[at8(me)]
        go(mine, mine, gl_ss.at[j], gl_rs.at[j], d=dp_peer(j))

    for j in range(1, n_dp):
        copy(ids_s.at[at8(me)], ids_r.at[at8(dp_peer(n_dp - j))],
             id_ss.at[j], id_rs.at[j], d=dp_peer(n_dp - j)).wait_recv()
    tally = jnp.zeros((1, group), F32)
    for k in range(n_dp):
        row = ids_r[pl.ds(k * 8, 1), :]
        col = to_col(row, cap)
        part = jnp.where(col == iota((cap, group), 1).astype(F32), 1.0, 0.0)
        mt[pl.ds(k * cap, cap), :] = part.astype(BF16)
        tally = tally + jnp.sum(part, axis=0, keepdims=True)
        if cap % 128 == 0:
            hit = row == iota((group, cap), 0).astype(F32)
            m[:, pl.ds(k * cap, cap)] = jnp.where(hit, 1.0, 0.0).astype(BF16)
    for k in range(n_cent):
        cnt_s[pl.ds(k * 8, 8), :] = jnp.broadcast_to(tally[:, k * fine : (k + 1) * fine], (8, fine))
    for j in range(1, n_cent):
        go(cnt_s.at[at8(reverse(cent_peer(j)))], cnt_r.at[pl.ds(j * 8, 8)],
           cnt_ss.at[j], cnt_rs.at[j], z=cent_peer(j))

    acc[...] = jnp.zeros_like(acc)

    def fine_counts():
        for j in range(1, n_cent):
            copy(cnt_s.at[at8(place)], cnt_r.at[pl.ds(j * 8, 8)],
                 cnt_ss.at[j], cnt_rs.at[j], z=cent_peer(n_cent - j)).wait_recv()
        total = cnt_s[at8(place), :]
        for j in range(1, n_cent):
            total = total + cnt_r[pl.ds(j * 8, 8), :]
        fine_scale = jnp.maximum(to_col(total[0:1, :], fine), 1.0)
        return fine_scale

    def coarse_members():
        for j in range(1, n_dp):
            copy(glab.at[at8(me)], glab.at[at8(dp_peer(n_dp - j))],
                 gl_ss.at[j], gl_rs.at[j], d=dp_peer(n_dp - j)).wait_recv()
        coarse_tally = jnp.zeros((block, 1), F32)
        for k in range(n_dp):
            row = glab[pl.ds(k * 8, 1), :]
            part = jnp.where(row == iota((block, rows2), 0).astype(F32), 1.0, 0.0)
            g[:, pl.ds(k * rows2, rows2)] = part.astype(BF16)
            coarse_tally = coarse_tally + jnp.sum(part, axis=1, keepdims=True)
        coarse_scale = jnp.maximum(coarse_tally, 1.0)
        return coarse_scale

    def cent_partner(b):
        return mz + (1 - 2 * ((mz // (1 << b)) % 2)) * (1 << b)

    def keep(b):
        size = n_cent >> b
        return (place // size) * size

    def rs_parts(c, b):
        return (rs_out[b].at[c], rs_in[b].at[c], rs_ss.at[c, b], rs_rs.at[c, b])

    def rs_send(c, b):
        half = n_cent >> (b + 1)
        other = 2 * keep(b) + half - keep(b + 1)
        rs_out[b][c] = pf[c % live, pl.ds(pl.multiple_of(other * fine, fine), half * fine), :].astype(BF16)
        go(*rs_parts(c, b), z=cent_partner(b))

    def rs_add(c, b):
        half = n_cent >> (b + 1)
        copy(*rs_parts(c, b), z=cent_partner(b)).wait_recv()
        mine = pl.ds(pl.multiple_of(keep(b + 1) * fine, fine), half * fine)
        pf[c % live, mine, :] += rs_in[b][c].astype(F32)

    def ag_send(c):
        mine = cz.at[c, span(place, fine)]
        for j in range(1, n_cent):
            go(mine, mine, ag_ss.at[c, j], ag_rs.at[c, j], z=cent_peer(j))

    def ag_wait(c):
        for j in range(1, n_cent):
            source = cent_peer(n_cent - j)
            theirs = cz.at[c, span(reverse(source), fine)]
            copy(theirs, theirs, ag_ss.at[c, j], ag_rs.at[c, j], z=source).wait_recv()

    def sums(c):
        for j in range(1, n_dp):
            source = dp_peer(n_dp - j)
            copy(send.at[c, span(me, cap)], recv.at[c, span(source, cap)],
                 a_ss.at[c, j], a_rs.at[c, j], d=source).wait_recv()
        if c + AHEAD < chunks:
            dispatch(c + AHEAD)
        if cap % 128 == 0:
            pf[c % live] = jnp.dot(m[...], recv[c], preferred_element_type=F32)
        else:
            pf[c % live] = lax.dot_general(mt[...], recv[c], (((0,), (0,)), ((), ())),
                                    preferred_element_type=F32)
        rs_send(c, 0)

    def halve(b, c):
        rs_add(c, b - 1)
        rs_send(c, b)

    def centroids(c):
        rs_add(c, bits - 1)
        value = (pf[c % live, span(place, fine), :] / fine_scale).astype(BF16)
        cz[c, span(place, fine), :] = value
        fine_out[:, pl.ds(c * w, w)] = value
        ag_send(c)

    def g_rows(c, d):
        return gr.at[c, span(d, rows2)]

    def g_args(c, k, d):
        return (g_rows(c, d), g_rows(c, d), g_ss.at[c, k], g_rs.at[c, k])

    if n_dp == 8:
        core = me % 2
        dx = (1 - 2 * ((me // 2) % 2)) * 2
        dy = (1 - 2 * ((me // 4) % 2)) * 4
        d1 = (1 - core) * dx + core * dy
        d2 = (1 - core) * dy + core * dx
        d3 = 1 - 2 * core

    def pick_rows(c):
        ag_wait(c)
        mine = jnp.zeros((rows2, w), F32)
        for k in range(n_cent):
            mine = mine + jnp.dot(pick[k], cz[c, pl.ds(k * fine, fine), :], preferred_element_type=F32)
        gr[c, span(me, rows2), :] = mine.astype(BF16)
        if n_dp == 8:
            go(*g_args(c, 0, me), d=me + d1)
            go(*g_args(c, 1, me), d=me + d2)
            go(*g_args(c, 2, me), d=me + d3)
        else:
            for j in range(1, n_dp):
                go(*g_args(c, j, me), d=dp_peer(j))
        near = jnp.dot(mt[...], cz[c], preferred_element_type=F32)
        gap = jnp.square(recv[c].astype(F32) - near)
        acc[...] += sum(gap[:, i : i + 128] for i in range(0, w, 128))
        if c == chunks - 1:
            for k in range(n_dp):
                col = jnp.sum(acc[pl.ds(k * cap, cap), :], axis=1, keepdims=True) / width
                sp_s[pl.ds(k * 8, 8), :] = jnp.broadcast_to(to_row(col, lanes), (8, lanes))
            for j in range(1, n_dp):
                go(sp_s.at[at8(dp_peer(j))], sp_r.at[at8(me)], sp_ss.at[j], sp_rs.at[j], d=dp_peer(j))
            sp_r[at8(me), :] = sp_s[at8(me), :]

    def forward_one(c):
        if n_dp == 8:
            copy(*g_args(c, 0, me + d1), d=me + d1).wait_recv()
            go(*g_args(c, 3, me + d1), d=me + d2)
            go(*g_args(c, 4, me + d1), d=me + d3)
            copy(*g_args(c, 1, me + d2), d=me + d2).wait_recv()
            go(*g_args(c, 5, me + d2), d=me + d3)

    def forward_two(c):
        if n_dp == 8:
            copy(*g_args(c, 3, me + d1 + d2), d=me + d2).wait_recv()
            go(*g_args(c, 6, me + d1 + d2), d=me + d3)

    def finish(c):
        if n_dp == 8:
            copy(*g_args(c, 2, me + d3), d=me + d3).wait_recv()
            copy(*g_args(c, 4, me + d3 + d2), d=me + d3).wait_recv()
            copy(*g_args(c, 5, me + d3 + d1), d=me + d3).wait_recv()
            copy(*g_args(c, 6, me + d3 + d1 + d2), d=me + d3).wait_recv()
        else:
            for j in range(1, n_dp):
                source = dp_peer(n_dp - j)
                copy(*g_args(c, j, source), d=source).wait_recv()
        result = jnp.dot(g[...], gr[c], preferred_element_type=F32)
        coarse_out[:, pl.ds(c * w, w)] = (result / coarse_scale).astype(BF16)

    stages = [sums]
    stages += [functools.partial(halve, b) for b in range(1, bits)]
    stages += [centroids]
    stages += [pick_rows, forward_one, forward_two, finish]
    for tick in range(chunks + len(stages) - 1):
        for s in reversed(range(len(stages))):
            if 0 <= tick - s < chunks:
                stages[s](tick - s)
        if tick == 0:
            fine_scale = fine_counts()
        if tick == 1:
            coarse_scale = coarse_members()

    for j in range(1, n_dp):
        source = dp_peer(n_dp - j)
        copy(sp_s.at[at8(me)], sp_r.at[at8(source)], sp_ss.at[j], sp_rs.at[j], d=source).wait_recv()
    spread = jnp.zeros((1, p_rows), F32)
    for k in range(n_dp):
        col = to_col(sp_r[pl.ds(k * 8, 1), :], cap)
        slots = (iota((cap, p_rows), 0) + k * cap).astype(F32)
        spread = spread + jnp.sum(jnp.where(slots == slot_row, col, 0.0), axis=0, keepdims=True)
    spread_out[...] = spread
    for made in started:
        made.wait_send()


def place_results(*refs):
    n = 3
    ins, outs, held, (sem_in, sem_out) = refs[:n], refs[n : 2 * n], refs[2 * n : 3 * n], refs[3 * n :]
    parts = []
    for i in (2, 1, 0):
        count = PARTS if i == 2 else 1
        rows = ins[i].shape[0] // count
        parts += [(i, pl.ds(k * rows, rows)) for k in range(count)]
    first = [
        pltpu.make_async_copy(ins[i].at[at], held[i].at[at], sem_in.at[k])
        for k, (i, at) in enumerate(parts)
    ]
    second = [
        pltpu.make_async_copy(held[i].at[at], outs[i].at[at], sem_out.at[k])
        for k, (i, at) in enumerate(parts)
    ]
    for move in first:
        move.start()
    for k, move in enumerate(first):
        move.wait()
        second[k].start()
    for move in second:
        move.wait()


def body(points, fine_assign, coarse_assign):
    n_dp = lax.axis_size("dp")
    n_cent = lax.axis_size("cent")
    p_rows, width = points.shape
    fine = coarse_assign.shape[0]
    sources = n_dp * n_cent
    cap = max(2, 2 * p_rows // sources) * n_cent
    cap2 = max(2, 2 * fine // n_cent)
    block = COARSE // n_cent
    w = width // CHUNKS
    bits = log2(n_cent)
    group, slots, rows2, lanes = n_cent * fine, n_dp * cap, n_cent * cap2, max(cap, 128)
    cfg = (n_dp, n_cent, p_rows, fine, width, w, cap, cap2, block)
    halves = [pltpu.VMEM((CHUNKS, (n_cent >> (b + 1)) * fine, w), BF16) for b in range(bits)]
    dma = pltpu.SemaphoreType.DMA
    scratch = [
        pltpu.VMEM((slots, p_rows), BF16),
        pltpu.VMEM((CHUNKS, slots, w), BF16),
        pltpu.VMEM((CHUNKS, slots, w), BF16),
        pltpu.VMEM((slots, group), BF16),
        pltpu.VMEM((group, slots) if cap % 128 == 0 else (16, 128), BF16),
        pltpu.VMEM((bits + 1, group, w), F32),
        pltpu.VMEM((CHUNKS, group, w), BF16),
        pltpu.VMEM((CHUNKS, n_dp * rows2, w), BF16),
        pltpu.VMEM((block, n_dp * rows2), BF16),
        pltpu.VMEM((n_dp * 8, lanes), F32),
        pltpu.VMEM((n_dp * 8, lanes), F32),
        pltpu.VMEM((n_cent * 8, fine), I32),
        pltpu.VMEM((n_dp * 8, rows2), F32),
        pltpu.VMEM((n_cent * 8, fine), F32),
        pltpu.VMEM((n_cent * 8, fine), F32),
        pltpu.VMEM((n_dp * 8, lanes), F32),
        pltpu.VMEM((n_dp * 8, lanes), F32),
        pltpu.VMEM((slots, 128), F32),
        *halves,
        *halves,
        dma((CHUNKS, n_dp)), dma((CHUNKS, n_dp)),
        dma((CHUNKS, bits)), dma((CHUNKS, bits)),
        dma((CHUNKS, n_cent)), dma((CHUNKS, n_cent)),
        dma((CHUNKS, n_dp)), dma((CHUNKS, n_dp)),
        dma((n_dp,)), dma((n_dp,)),
        dma((n_cent,)), dma((n_cent,)),
        dma((n_cent,)), dma((n_cent,)),
        dma((n_dp,)), dma((n_dp,)),
        dma((n_dp,)), dma((n_dp,)),
    ]
    vmem = pl.BlockSpec(memory_space=pltpu.VMEM)
    results = pl.pallas_call(
        functools.partial(kernel, cfg),
        out_shape=(
            jax.ShapeDtypeStruct((1, p_rows), F32),
            jax.ShapeDtypeStruct((fine, width), BF16),
            jax.ShapeDtypeStruct((block, width), BF16),
        ),
        in_specs=[vmem] * 3,
        out_specs=(vmem,) * 3,
        scratch_shapes=scratch,
        compiler_params=pltpu.CompilerParams(
            collective_id=0, has_side_effects=True, vmem_limit_bytes=60 * 1024 * 1024
        ),
        cost_estimate=pl.CostEstimate(
            flops=2 * width * (slots * (p_rows + 2 * group) + block * n_dp * rows2),
            bytes_accessed=2 * width * (p_rows + fine + block),
            transcendentals=0,
        ),
    )(points, fine_assign.reshape(1, p_rows), coarse_assign.reshape(1, fine))
    anywhere = pl.BlockSpec(memory_space=pl.ANY)
    spread, fine_centroids, coarse_centroids = pl.pallas_call(
        place_results,
        out_shape=tuple(jax.ShapeDtypeStruct(r.shape, r.dtype) for r in results),
        in_specs=[anywhere] * 3,
        out_specs=(anywhere,) * 3,
        scratch_shapes=[
            *(pltpu.VMEM(r.shape, r.dtype) for r in results),
            dma((PARTS + 2,)),
            dma((PARTS + 2,)),
        ],
    )(*results)
    return (spread.reshape(p_rows), fine_centroids, coarse_centroids)


def solution(mesh):
    placed = (P(("dp", "cent"), None), P(("dp", "cent")), P(("dp", "cent")))
    return jax.shard_map(
        body,
        mesh=mesh,
        in_specs=placed,
        out_specs=(P(("dp", "cent")), P(("dp", "cent"), None), P("cent", None)),
        check_vma=False,
    )
```
